32 devices in a mesh: dp: 32 (over z, y, x, core), tensor: 1.
Axes of the slice: x: 2, y: 2, z: 4, core: 2. Of those that a mesh axis runs over, the one named last changes fastest.
Arguments:
- hidden_in: bfloat16 [8192, 8192], P('dp', 'tensor'), may hold values from -6 to 6
- query_weight: bfloat16 [128, 8192], P('tensor'), may hold values from -0.0625 to 0.0625
- saved_keys: bfloat16 [8192, 64], P('dp', 'tensor'), may hold values from -128 to 128
- saved_values: bfloat16 [8192, 64], P('dp', 'tensor'), may hold values from -6 to 6
- grad_out: bfloat16 [8192, 128], P('dp', 'tensor'), may hold values from -6 to 6
Outputs:
- grad_query_weight: bfloat16 [128, 8192], P('tensor')
- grad_hidden: bfloat16 [8192, 8192], P('dp', 'tensor')
The draws below stay inside these ranges and needn't reach their ends.
All inputs are finite; a program needn't handle non-finite values.
Results may differ from the reference program's by a relative error of at most 0.035.
The reference program's roundings to bfloat16 on the way (of `query`, `grad_score` and `grad_query`) count: a program that leaves them out, or rounds other values in their place, can miss the bound.
Values may be sent and summed in bfloat16 or wider, within the bound.
No kernel may reach another device: no remote copies, remote signals or barrier semaphores. Data moves between devices by JAX's collectives and lax.ppermute only.
A program may use at most 64 MiB of HBM per device.

```python
import jax
import jax.numpy as jnp
from jax import lax

D = 8192
HEAD = 64
QH = 2
TOK_DEV = 256
KV_HEADS = 1
HEADS = 2
TOKENS = 8192
N_DP = 32
N_TENSOR = 1


def draw_saved_keys(key, part):
    key = jax.random.fold_in(key, 11)
    normal_draw = jnp.clip(jax.random.normal(key, (TOKENS, KV_HEADS * HEAD), jnp.float32), -4.0, 4.0)
    return normal_draw.astype(jnp.bfloat16)


def levels(rng, dims, split, least, top_value):
    level, own = 1.0, jax.random.fold_in(rng, 6)
    for axis_at, blocks in split:
        draws = jnp.exp(jax.random.uniform(jax.random.fold_in(own, axis_at), (blocks,), jnp.float32, least / len(split), top_value / len(split)))
        level = level * jnp.repeat(draws, dims[axis_at] // blocks).reshape([-1 if axis == axis_at else 1 for axis in range(len(dims))])
    return level


def centred(rng, shape, scale, reach, cuts=(), held_as=jnp.bfloat16):
    factor_of = levels(rng, shape, cuts, -0.22, 0.18) if cuts else 1.0
    values = jax.random.normal(rng, shape, jnp.float32) * scale * factor_of
    return jnp.minimum(jnp.maximum(values, -reach), reach).astype(held_as)


def setup_inputs(seed: int = 0) -> dict:
    streams_of = jax.random.split(jax.random.key(seed), 6)
    hidden_in = centred(streams_of[0], (TOKENS, D), 1.0, 6.0, ((0, 32),))
    query_weight = centred(streams_of[1], (HEADS * HEAD, D), D ** -0.5, 0.0625)
    saved_keys = draw_saved_keys(jax.random.fold_in(streams_of[5], 71), 0)
    saved_values = centred(streams_of[3], (TOKENS, KV_HEADS * HEAD), 1.0, 6.0, ((0, 32),))
    grad_out = centred(streams_of[4], (TOKENS, HEADS * HEAD), 0.5, 6.0, ((0, 32),))
    return {"hidden_in": hidden_in, "query_weight": query_weight, "saved_keys": saved_keys, "saved_values": saved_values, "grad_out": grad_out}


def head_grad(query, keys, values, grad_out):
    length = query.shape[0]
    score_scale = query.shape[1] ** (-0.5)
    scores = jnp.einsum('qd,kd->qk', query.astype(jnp.float32), keys.astype(jnp.float32)) * score_scale
    row_index = jnp.arange(length)[:, None]
    col_index = jnp.arange(length)[None, :]
    causal_mask = col_index <= row_index
    scores = jnp.where(causal_mask, scores, -1e+30)
    row_peak = lax.optimization_barrier(jnp.max(scores, axis=1, keepdims=True))
    raised = jnp.where(causal_mask, jnp.exp(scores - row_peak), 0.0)
    attn_weights = raised / lax.optimization_barrier(jnp.sum(raised, axis=1, keepdims=True))
    grad_prob = jnp.einsum('qd,kd->qk', grad_out.astype(jnp.float32), values.astype(jnp.float32))
    row_delta = lax.optimization_barrier(jnp.sum(attn_weights * grad_prob, axis=1, keepdims=True))
    grad_score = (attn_weights * (grad_prob - row_delta) * score_scale).astype(jnp.bfloat16)
    return jnp.dot(grad_score, keys, preferred_element_type=jnp.float32).astype(jnp.bfloat16)

def group_grad(query, keys, values, grad_out):
    head_size = keys.shape[1]
    count = query.shape[1] // head_size
    pieces = [head_grad(query[:, i * head_size:(i + 1) * head_size], keys, values, grad_out[:, i * head_size:(i + 1) * head_size]) for i in range(count)]
    return jnp.concatenate(pieces, axis=1)

def by_groups(array, width):
    shaped = array.reshape(N_DP, TOK_DEV, N_TENSOR, width).transpose(0, 2, 1, 3)
    return shaped.reshape(N_DP * N_TENSOR, TOK_DEV, width)

def reference(hidden_in, query_weight, saved_keys, saved_values, grad_out):
    group_width = QH * HEAD
    query = jnp.dot(hidden_in, query_weight.T, preferred_element_type=jnp.float32).astype(jnp.bfloat16)
    grads = lax.map(lambda packed: group_grad(packed[0], packed[1], packed[2], packed[3]), (by_groups(query, group_width), by_groups(saved_keys, HEAD), by_groups(saved_values, HEAD), by_groups(grad_out, group_width)))
    grad_query = grads.reshape(N_DP, N_TENSOR, TOK_DEV, group_width).transpose(0, 2, 1, 3).reshape(TOKENS, N_TENSOR * group_width)
    grad_query_weight = jnp.dot(grad_query.T, hidden_in, preferred_element_type=jnp.float32).astype(jnp.bfloat16)
    grad_groups = grad_query.reshape(TOKENS, N_TENSOR, group_width).transpose(1, 0, 2)
    weight_groups = query_weight.reshape(N_TENSOR, group_width, D)

    def add_group(running, packed):
        group_part = jnp.dot(packed[0], packed[1], preferred_element_type=jnp.float32)
        rounded = lax.optimization_barrier(group_part.astype(jnp.bfloat16))
        return (running + rounded.astype(jnp.float32), None)
    summed, unused = lax.scan(add_group, jnp.zeros((TOKENS, D), jnp.float32), (grad_groups, weight_groups))
    return (grad_query_weight, summed.astype(jnp.bfloat16))
```

```python
import jax
import jax.numpy as jnp
from jax import lax
from jax.sharding import PartitionSpec as P


def head_grad(query, keys, values, grad_out):
    length = query.shape[0]
    score_scale = query.shape[1] ** (-0.5)
    scores = jnp.einsum("qd,kd->qk", query, keys, preferred_element_type=jnp.float32) * score_scale
    row_index = jnp.arange(length)[:, None]
    col_index = jnp.arange(length)[None, :]
    causal_mask = col_index <= row_index
    scores = jnp.where(causal_mask, scores, -1e30)
    row_peak = jnp.max(scores, axis=1, keepdims=True)
    raised = jnp.where(causal_mask, jnp.exp(scores - row_peak), 0.0)
    attn_weights = raised / jnp.sum(raised, axis=1, keepdims=True)
    grad_prob = jnp.einsum("qd,kd->qk", grad_out, values, preferred_element_type=jnp.float32)
    row_delta = jnp.sum(attn_weights * grad_prob, axis=1, keepdims=True)
    grad_score = (attn_weights * (grad_prob - row_delta) * score_scale).astype(jnp.bfloat16)
    return jnp.dot(grad_score, keys, preferred_element_type=jnp.float32).astype(jnp.bfloat16)


def group_grad(query, keys, values, grad_out):
    head_size = keys.shape[1]
    count = query.shape[1] // head_size
    pieces = [
        head_grad(
            query[:, i * head_size : (i + 1) * head_size],
            keys,
            values,
            grad_out[:, i * head_size : (i + 1) * head_size],
        )
        for i in range(count)
    ]
    return jnp.concatenate(pieces, axis=1)


def stages_of(count):
    bits = count.bit_length() - 1
    return [(0, 1)] + [(low, min(low + 3, bits)) for low in range(1, bits, 3)]


def add_over_devices(blocks, count):
    swap = lambda array, step: lax.ppermute(array, "dp", [(i, i ^ step) for i in range(count)])
    stages = stages_of(count)
    total = blocks
    for low, high in stages:
        ways = 1 << (high - low)
        parts = total.reshape(-1, ways, *total.shape[1:])
        arrived = [swap(parts[:, way], way << low) for way in range(1, ways)]
        added = parts[:, 0].astype(jnp.float32)
        for piece in arrived:
            added = added + piece.astype(jnp.float32)
        total = added.astype(jnp.bfloat16)
    for low, high in reversed(stages):
        ways = 1 << (high - low)
        pieces = [total] + [swap(total, way << low) for way in range(1, ways)]
        total = jnp.stack(pieces, axis=1).reshape(-1, *total.shape[1:])
    return total


def per_device(count, hidden_in, query_weight, saved_keys, saved_values, grad_out):
    whole_in = lax.all_gather(hidden_in, "tensor", axis=1, tiled=True)
    query = lax.dot_general(
        whole_in, query_weight, (((1,), (1,)), ((), ())), preferred_element_type=jnp.float32
    ).astype(jnp.bfloat16)
    grad_query = group_grad(query, saved_keys, saved_values, grad_out)
    grad_rows = lax.dot_general(
        grad_query, whole_in, (((0,), (0,)), ((), ())), preferred_element_type=jnp.float32
    ).astype(jnp.bfloat16)
    input_terms = jnp.dot(grad_query, query_weight, preferred_element_type=jnp.float32)
    grad_hidden = lax.psum_scatter(
        input_terms.astype(jnp.bfloat16), "tensor", scatter_dimension=1, tiled=True
    )
    rows, columns = grad_rows.shape
    order = jnp.arange(count) ^ lax.axis_index("dp")
    blocks = grad_rows.reshape(rows, count, columns // count).transpose(1, 0, 2)
    total = add_over_devices(blocks[order], count)
    grad_query_weight = total[order].transpose(1, 0, 2).reshape(rows, columns)
    return (grad_query_weight, grad_hidden)


def solution(mesh):
    count = mesh.shape["dp"]
    placed = (
        P("dp", "tensor"),
        P("tensor", None),
        P("dp", "tensor"),
        P("dp", "tensor"),
        P("dp", "tensor"),
    )
    return jax.shard_map(
        lambda *arrays: per_device(count, *arrays),
        mesh=mesh,
        in_specs=placed,
        out_specs=(P("tensor", None), P("dp", "tensor")),
        check_vma=False,
    )
```

```python
import functools

import jax
import jax.numpy as jnp
from jax import lax
from jax.experimental import pallas as pl
from jax.experimental.pallas import tpu as pltpu
from jax.sharding import PartitionSpec as P

VMEM_LIMIT = 40 * 1024 * 1024
ANY = pl.BlockSpec(memory_space=pl.ANY)
WHOLE = pl.BlockSpec(memory_space=pltpu.VMEM)


def dot_tt(left, right):
    return lax.dot_general(left, right, (((1,), (1,)), ((), ())), preferred_element_type=jnp.float32)


def head_grad(query, keys, values, grad_out):
    length, head_size = query.shape
    score_scale = head_size ** (-0.5)
    causal_mask = lax.broadcasted_iota(jnp.int32, (length, length), 1) <= lax.broadcasted_iota(
        jnp.int32, (length, length), 0
    )
    scores = jnp.where(causal_mask, dot_tt(query, keys) * score_scale, -1e30)
    raised = jnp.exp(scores - jnp.max(scores, axis=1, keepdims=True))
    attn_weights = raised * (1.0 / jnp.sum(raised, axis=1, keepdims=True))
    grad_prob = dot_tt(grad_out, values)
    row_delta = jnp.sum(attn_weights * grad_prob, axis=1, keepdims=True)
    grad_score = (attn_weights * (grad_prob - row_delta) * score_scale).astype(jnp.bfloat16)
    return jnp.dot(grad_score, keys, preferred_element_type=jnp.float32).astype(jnp.bfloat16)


def rows_kernel(
    blocks, core_ref, hidden_hbm, weight_hbm, keys_ref, values_ref, grad_out_ref,
    other_hbm, own_hbm, grad_query_ref,
    hidden, weight, other, own, hidden_sem, weight_sem, out_sem,
):
    tokens, width = hidden.shape
    rows = weight.shape[0]
    half, step = rows // 2, width // blocks
    head_size = keys_ref.shape[1]
    core = core_ref[0]
    copies = []
    for block in range(blocks):
        columns = pl.ds(block * step, step)
        from_hidden = pltpu.make_async_copy(hidden_hbm.at[:, columns], hidden.at[:, columns], hidden_sem.at[block])
        from_hidden.start()
        halves = []
        for place, source in enumerate((1 - core, core)):
            here = pl.ds(place * half, half)
            there = pl.ds(pl.multiple_of(source * half, half), half)
            copy = pltpu.make_async_copy(
                weight_hbm.at[there, columns], weight.at[here, columns], weight_sem.at[place, block]
            )
            copy.start()
            halves.append(copy)
        copies.append((from_hidden, *halves))
    total = jnp.zeros((tokens, rows), jnp.float32)
    for block in range(blocks):
        for copy in copies[block]:
            copy.wait()
        columns = pl.ds(block * step, step)
        total += dot_tt(hidden[:, columns], weight[:, columns])
    query = total.astype(jnp.bfloat16)
    keys, values = keys_ref[...], values_ref[...]
    given = grad_out_ref[...]
    first = core == 0
    given = jnp.concatenate(
        [
            jnp.where(first, given[:, half:], given[:, :half]),
            jnp.where(first, given[:, :half], given[:, half:]),
        ],
        axis=1,
    )
    grads = jnp.concatenate(
        [
            head_grad(query[:, low : low + head_size], keys, values, given[:, low : low + head_size])
            for low in range(0, rows, head_size)
        ],
        axis=1,
    )
    grad_query_ref[...] = jnp.concatenate(
        [
            jnp.where(first, grads[:, half:], grads[:, :half]),
            jnp.where(first, grads[:, :half], grads[:, half:]),
        ],
        axis=1,
    )
    turned = grads.T
    sent = []
    for block in range(blocks):
        columns = pl.ds(block * step, step)
        term = jnp.dot(turned, hidden[:, columns], preferred_element_type=jnp.float32).astype(jnp.bfloat16)
        other[block] = term[:half]
        own[block] = term[half:]
        for place, (buffer, target) in enumerate(((other, other_hbm), (own, own_hbm))):
            copy = pltpu.make_async_copy(buffer.at[block], target.at[block], out_sem.at[place, block])
            copy.start()
            sent.append(copy)
    for copy in sent:
        copy.wait()


def rows_of(blocks, core, hidden_in, query_weight, saved_keys, saved_values, grad_out):
    tokens, width = hidden_in.shape
    rows = query_weight.shape[0]
    piece = (blocks, rows // 2, width // blocks)
    return pl.pallas_call(
        functools.partial(rows_kernel, blocks),
        out_shape=(
            jax.ShapeDtypeStruct(piece, jnp.bfloat16),
            jax.ShapeDtypeStruct(piece, jnp.bfloat16),
            jax.ShapeDtypeStruct((tokens, rows), jnp.bfloat16),
        ),
        in_specs=[pl.BlockSpec(memory_space=pltpu.SMEM), ANY, ANY, WHOLE, WHOLE, WHOLE],
        out_specs=(ANY, ANY, WHOLE),
        scratch_shapes=[
            pltpu.VMEM((tokens, width), jnp.bfloat16),
            pltpu.VMEM((rows, width), jnp.bfloat16),
            pltpu.VMEM(piece, jnp.bfloat16),
            pltpu.VMEM(piece, jnp.bfloat16),
            pltpu.SemaphoreType.DMA((blocks,)),
            pltpu.SemaphoreType.DMA((2, blocks)),
            pltpu.SemaphoreType.DMA((2, blocks)),
        ],
        compiler_params=pltpu.CompilerParams(vmem_limit_bytes=VMEM_LIMIT),
        cost_estimate=pl.CostEstimate(
            flops=4 * tokens * width * rows,
            bytes_accessed=2 * (tokens * width + 2 * rows * width),
            transcendentals=tokens * tokens * 2,
        ),
    )(core, hidden_in, query_weight, saved_keys, saved_values, grad_out)


def assemble_kernel(core_ref, own_hbm, other_hbm, out_hbm, sem):
    blocks, half, step = own_hbm.shape
    core = core_ref[0]
    copies = []
    for place, (source, rows) in enumerate(((own_hbm, core), (other_hbm, 1 - core))):
        there = pl.ds(pl.multiple_of(rows * half, half), half)
        for block in range(blocks):
            copy = pltpu.make_async_copy(
                source.at[block], out_hbm.at[there, pl.ds(block * step, step)], sem.at[place, block]
            )
            copy.start()
            copies.append(copy)
    for copy in copies:
        copy.wait()


def assemble(core, own, other):
    blocks, half, step = own.shape
    return pl.pallas_call(
        assemble_kernel,
        out_shape=jax.ShapeDtypeStruct((2 * half, blocks * step), jnp.bfloat16),
        in_specs=[pl.BlockSpec(memory_space=pltpu.SMEM), ANY, ANY],
        out_specs=ANY,
        scratch_shapes=[pltpu.SemaphoreType.DMA((2, blocks))],
        compiler_params=pltpu.CompilerParams(vmem_limit_bytes=VMEM_LIMIT),
        cost_estimate=pl.CostEstimate(flops=0, bytes_accessed=8 * half * blocks * step, transcendentals=0),
    )(core, own, other)


def swap(array, step, count):
    return lax.ppermute(array, "dp", [(i, i ^ step) for i in range(count)])


def add(left, right):
    return (left.astype(jnp.float32) + right.astype(jnp.float32)).astype(jnp.bfloat16)


def per_device(count, hidden_in, query_weight, saved_keys, saved_values, grad_out):
    bits = count.bit_length() - 1
    wide = min(3, bits - 1)
    blocks = 1 << wide
    groups = [
        [high << (wide + 1) | (place ^ (high & 1) * (blocks >> 1)) << 1 | core for place in range(blocks)]
        for high in range(count >> (wide + 1))
        for core in range(2)
    ]
    if hidden_in.shape[1] != query_weight.shape[1]:
        hidden_in = lax.all_gather(hidden_in, "tensor", axis=1, tiled=True)
    core = (lax.axis_index("dp") & 1).astype(jnp.int32).reshape(1)
    other, own, grad_query = rows_of(
        blocks, core, hidden_in, query_weight, saved_keys, saved_values, grad_out
    )
    chip = add(own, swap(other, 1, count))
    parts = lax.all_to_all(chip, "dp", 0, 0, axis_index_groups=groups)
    total = jnp.sum(parts.astype(jnp.float32), axis=0).astype(jnp.bfloat16)
    grad_query, total = lax.optimization_barrier((grad_query, total))
    input_terms = jnp.dot(grad_query, query_weight, preferred_element_type=jnp.float32)
    grad_hidden = lax.psum_scatter(
        input_terms.astype(jnp.bfloat16), "tensor", scatter_dimension=1, tiled=True
    )
    for bit in range(wide + 1, bits):
        total = add(total, swap(total, 3 << wide if bit == wide + 1 else 1 << bit, count))
    copies = jnp.broadcast_to(total[None], (blocks, *total.shape))
    gathered = lax.all_to_all(copies, "dp", 0, 0, axis_index_groups=groups)
    grad_query_weight = assemble(core, gathered, swap(gathered, 1, count))
    return (grad_query_weight, grad_hidden)


def solution(mesh):
    count = mesh.shape["dp"]
    placed = (
        P("dp", "tensor"),
        P("tensor", None),
        P("dp", "tensor"),
        P("dp", "tensor"),
        P("dp", "tensor"),
    )
    return jax.shard_map(
        functools.partial(per_device, count),
        mesh=mesh,
        in_specs=placed,
        out_specs=(P("tensor", None), P("dp", "tensor")),
        check_vma=False,
    )
```

```python
import functools

import jax
import jax.numpy as jnp
from jax import lax
from jax.experimental import pallas as pl
from jax.experimental.pallas import tpu as pltpu
from jax.sharding import PartitionSpec as P

VMEM_LIMIT = 40 * 1024 * 1024
ANY = pl.BlockSpec(memory_space=pl.ANY)
SCALAR = pl.BlockSpec(memory_space=pltpu.SMEM)


def dot(left, right):
    return jnp.dot(left, right, preferred_element_type=jnp.float32)


def dot_tt(left, right):
    return lax.dot_general(left, right, (((1,), (1,)), ((), ())), preferred_element_type=jnp.float32)


def head_grad(query, keys, values, grad_out):
    head_size, length = keys.shape
    score_scale = head_size ** (-0.5)
    causal_mask = lax.broadcasted_iota(jnp.int32, (length, length), 1) <= lax.broadcasted_iota(
        jnp.int32, (length, length), 0
    )
    scores = jnp.where(causal_mask, dot(query, keys) * score_scale, -1e30)
    raised = jnp.exp(scores - jnp.max(scores, axis=1, keepdims=True))
    attn_weights = raised * (1.0 / jnp.sum(raised, axis=1, keepdims=True))
    grad_prob = dot(grad_out, values)
    row_delta = jnp.sum(attn_weights * grad_prob, axis=1, keepdims=True)
    grad_score = (attn_weights * (grad_prob - row_delta) * score_scale).astype(jnp.bfloat16)
    return dot_tt(grad_score, keys).astype(jnp.bfloat16)


def turned_round(first, array):
    half = array.shape[1] // 2
    low, high = array[:, :half], array[:, half:]
    return jnp.concatenate([jnp.where(first, low, high), jnp.where(first, high, low)], axis=1)


def query_kernel(
    blocks, core_ref, hidden_hbm, weight_hbm, keys_hbm, values_hbm, grad_out_hbm,
    other_hbm, grad_query_hbm,
    hidden, weight, keys, values, grad_out, other, grad_query, hidden_sem, weight_sem, small_sem, out_sem,
):
    tokens, width = hidden.shape
    rows = weight.shape[0]
    head_size = keys.shape[0]
    step = width // blocks
    core = core_ref[0]
    copies = []
    for block in range(blocks):
        columns = pl.ds(block * step, step)
        pair = [
            pltpu.make_async_copy(weight_hbm.at[:, columns], weight.at[:, columns], weight_sem.at[block]),
            pltpu.make_async_copy(hidden_hbm.at[:, columns], hidden.at[:, columns], hidden_sem.at[block]),
        ]
        for copy in pair:
            copy.start()
        copies.append(pair)
    small = [
        pltpu.make_async_copy(source, target, small_sem.at[place])
        for place, (source, target) in enumerate(
            ((keys_hbm, keys), (values_hbm, values), (grad_out_hbm, grad_out))
        )
    ]
    for copy in small:
        copy.start()
    total = jnp.zeros((tokens, rows), jnp.float32)
    for block in range(blocks):
        for copy in copies[block]:
            copy.wait()
        columns = pl.ds(block * step, step)
        total += dot_tt(hidden[:, columns], weight[:, columns])
    query = total.astype(jnp.bfloat16)
    for copy in small:
        copy.wait()
    given = grad_out[...]
    grads = jnp.concatenate(
        [
            head_grad(
                query[:, low : low + head_size], keys[...], values[...], given[:, low : low + head_size]
            )
            for low in range(0, rows, head_size)
        ],
        axis=1,
    )
    grad_query[...] = grads
    sent = [pltpu.make_async_copy(grad_query, grad_query_hbm, small_sem.at[3])]
    sent[0].start()
    half = rows // 2
    turned = jnp.where(core == 0, grads[:, half:], grads[:, :half]).T
    for block in range(blocks):
        term = dot(turned, hidden[:, pl.ds(block * step, step)])
        other[block] = term.astype(jnp.bfloat16)
        sent.append(pltpu.make_async_copy(other.at[block], other_hbm.at[block], out_sem.at[block]))
        sent[-1].start()
    for copy in sent:
        copy.wait()


def query_and_other(blocks, core, hidden_in, query_weight, keys, values, grad_out):
    tokens, width = hidden_in.shape
    rows = query_weight.shape[0]
    piece = (blocks, rows // 2, width // blocks)
    like = lambda array: pltpu.VMEM(array.shape, array.dtype)
    return pl.pallas_call(
        functools.partial(query_kernel, blocks),
        out_shape=(
            jax.ShapeDtypeStruct(piece, jnp.bfloat16),
            jax.ShapeDtypeStruct((tokens, rows), jnp.bfloat16),
        ),
        in_specs=[SCALAR] + [ANY] * 5,
        out_specs=(ANY, ANY),
        scratch_shapes=[
            like(hidden_in),
            like(query_weight),
            like(keys),
            like(values),
            like(grad_out),
            pltpu.VMEM(piece, jnp.bfloat16),
            pltpu.VMEM((tokens, rows), jnp.bfloat16),
            pltpu.SemaphoreType.DMA((blocks,)),
            pltpu.SemaphoreType.DMA((blocks,)),
            pltpu.SemaphoreType.DMA((4,)),
            pltpu.SemaphoreType.DMA((blocks,)),
        ],
        compiler_params=pltpu.CompilerParams(vmem_limit_bytes=VMEM_LIMIT),
        cost_estimate=pl.CostEstimate(
            flops=3 * tokens * width * rows,
            bytes_accessed=2 * (tokens * width + rows * width),
            transcendentals=tokens * tokens * 2,
        ),
    )(core, *(pltpu.with_memory_space_constraint(x, pltpu.HBM) for x in (hidden_in, query_weight, keys, values, grad_out)))


def own_kernel(core_ref, grad_query_hbm, hidden_hbm, own_hbm, grad_query, hidden, own, in_sem, hidden_sem, out_sem):
    blocks, half, step = own.shape
    first = pltpu.make_async_copy(grad_query_hbm, grad_query, in_sem)
    first.start()
    copies = []
    for block in range(blocks):
        columns = pl.ds(block * step, step)
        copies.append(
            pltpu.make_async_copy(hidden_hbm.at[:, columns], hidden.at[:, columns], hidden_sem.at[block])
        )
        copies[-1].start()
    first.wait()
    turned = jnp.where(core_ref[0] == 0, grad_query[:, :half], grad_query[:, half:]).T
    sent = []
    for block in range(blocks):
        copies[block].wait()
        own[block] = dot(turned, hidden[:, pl.ds(block * step, step)]).astype(jnp.bfloat16)
        sent.append(pltpu.make_async_copy(own.at[block], own_hbm.at[block], out_sem.at[block]))
        sent[-1].start()
    for copy in sent:
        copy.wait()


def own_rows(blocks, core, grad_query, hidden_in):
    tokens, width = hidden_in.shape
    rows = grad_query.shape[1]
    piece = (blocks, rows // 2, width // blocks)
    return pl.pallas_call(
        own_kernel,
        out_shape=jax.ShapeDtypeStruct(piece, jnp.bfloat16),
        in_specs=[SCALAR, ANY, ANY],
        out_specs=ANY,
        scratch_shapes=[
            pltpu.VMEM((tokens, rows), jnp.bfloat16),
            pltpu.VMEM((tokens, width), jnp.bfloat16),
            pltpu.VMEM(piece, jnp.bfloat16),
            pltpu.SemaphoreType.DMA(()),
            pltpu.SemaphoreType.DMA((blocks,)),
            pltpu.SemaphoreType.DMA((blocks,)),
        ],
        compiler_params=pltpu.CompilerParams(vmem_limit_bytes=VMEM_LIMIT),
        cost_estimate=pl.CostEstimate(
            flops=tokens * width * rows, bytes_accessed=2 * tokens * width, transcendentals=0
        ),
    )(core, grad_query, pltpu.with_memory_space_constraint(hidden_in, pltpu.HBM))


def place_kernel(core_ref, piece_hbm, out_hbm, sem):
    blocks, half, step = piece_hbm.shape
    rows = pl.ds(pl.multiple_of(core_ref[0] * half, half), half)
    copies = [
        pltpu.make_async_copy(piece_hbm.at[block], out_hbm.at[rows, pl.ds(block * step, step)], sem.at[block])
        for block in range(blocks)
    ]
    for copy in copies:
        copy.start()
    for copy in copies:
        copy.wait()


def place_kernel_on(core_ref, piece_hbm, before_hbm, out_hbm, sem):
    place_kernel(core_ref, piece_hbm, out_hbm, sem)


def place(core, piece, before=None):
    blocks, half, step = piece.shape
    return pl.pallas_call(
        place_kernel if before is None else place_kernel_on,
        out_shape=jax.ShapeDtypeStruct((2 * half, blocks * step), jnp.bfloat16),
        in_specs=[SCALAR, ANY] + [ANY] * (before is not None),
        out_specs=ANY,
        scratch_shapes=[pltpu.SemaphoreType.DMA((blocks,))],
        input_output_aliases={} if before is None else {2: 0},
        compiler_params=pltpu.CompilerParams(vmem_limit_bytes=VMEM_LIMIT),
        cost_estimate=pl.CostEstimate(flops=0, bytes_accessed=4 * half * blocks * step, transcendentals=0),
    )(core, piece, *(() if before is None else (before,)))


def swap(array, step, count):
    return lax.ppermute(array, "dp", [(i, i ^ step) for i in range(count)])


def add(left, right):
    return (left.astype(jnp.float32) + right.astype(jnp.float32)).astype(jnp.bfloat16)


def per_device(count, hidden_in, query_weight, saved_keys, saved_values, grad_out):
    bits = count.bit_length() - 1
    wide = min(3, bits - 1)
    blocks = 1 << wide
    groups = [
        [high << (wide + 1) | (place ^ (high & 1) * (blocks >> 1)) << 1 | core for place in range(blocks)]
        for high in range(count >> (wide + 1))
        for core in range(2)
    ]
    if hidden_in.shape[1] != query_weight.shape[1]:
        hidden_in = lax.all_gather(hidden_in, "tensor", axis=1, tiled=True)
    core = (lax.axis_index("dp") & 1).astype(jnp.int32).reshape(1)
    other, grad_query = query_and_other(
        blocks, core, hidden_in, query_weight, saved_keys.T, saved_values.T, grad_out
    )
    arriving = swap(other, 1, count)
    own = own_rows(blocks, core, grad_query, hidden_in)
    chip = add(own, arriving)
    parts = lax.all_to_all(chip, "dp", 0, 0, axis_index_groups=groups)
    total = jnp.sum(parts.astype(jnp.float32), axis=0).astype(jnp.bfloat16)
    grad_query, total = lax.optimization_barrier((grad_query, total))
    input_terms = dot(grad_query, query_weight)
    grad_hidden = lax.psum_scatter(
        input_terms.astype(jnp.bfloat16), "tensor", scatter_dimension=1, tiled=True
    )
    for bit in range(wide + 1, bits):
        arriving = swap(total, 3 << wide if bit == wide + 1 else 1 << bit, count)
        if bit == wide + 1:
            arriving, grad_hidden = lax.optimization_barrier((arriving, grad_hidden))
        total = add(total, arriving)
    copies = jnp.broadcast_to(total[None], (blocks, *total.shape))
    gathered = lax.all_to_all(copies, "dp", 0, 0, axis_index_groups=groups)
    arriving = swap(gathered, 1, count)
    grad_query_weight = place(1 - core, arriving, place(core, gathered))
    return (grad_query_weight, grad_hidden)


def solution(mesh):
    count = mesh.shape["dp"]
    placed = (
        P("dp", "tensor"),
        P("tensor", None),
        P("dp", "tensor"),
        P("dp", "tensor"),
        P("dp", "tensor"),
    )
    return jax.shard_map(
        functools.partial(per_device, count),
        mesh=mesh,
        in_specs=placed,
        out_specs=(P("tensor", None), P("dp", "tensor")),
        check_vma=False,
    )
```

```python
import functools

import jax
import jax.numpy as jnp
from jax import lax
from jax.experimental import pallas as pl
from jax.experimental.pallas import tpu as pltpu
from jax.sharding import PartitionSpec as P

VMEM_LIMIT = 40 * 1024 * 1024
ANY = pl.BlockSpec(memory_space=pl.ANY)
SCALAR = pl.BlockSpec(memory_space=pltpu.SMEM)


def dot(left, right):
    return jnp.dot(left, right, preferred_element_type=jnp.float32)


def dot_tt(left, right):
    return lax.dot_general(left, right, (((1,), (1,)), ((), ())), preferred_element_type=jnp.float32)


def head_grad(query, keys, values, grad_out):
    head_size, length = keys.shape
    score_scale = head_size ** (-0.5)
    causal_mask = lax.broadcasted_iota(jnp.int32, (length, length), 1) <= lax.broadcasted_iota(
        jnp.int32, (length, length), 0
    )
    scores = jnp.where(causal_mask, dot(query, keys) * score_scale, -1e30)
    raised = jnp.exp(scores - jnp.max(scores, axis=1, keepdims=True))
    attn_weights = raised * (1.0 / jnp.sum(raised, axis=1, keepdims=True))
    grad_prob = dot(grad_out, values)
    row_delta = jnp.sum(attn_weights * grad_prob, axis=1, keepdims=True)
    grad_score = (attn_weights * (grad_prob - row_delta) * score_scale).astype(jnp.bfloat16)
    return dot_tt(grad_score, keys).astype(jnp.bfloat16)


def turned_round(first, array):
    half = array.shape[1] // 2
    low, high = array[:, :half], array[:, half:]
    return jnp.concatenate([jnp.where(first, low, high), jnp.where(first, high, low)], axis=1)


def query_kernel(
    blocks, core_ref, hidden_hbm, weight_hbm, keys_hbm, values_hbm, grad_out_hbm,
    other_hbm, grad_query_hbm,
    hidden, weight, keys, values, grad_out, other, grad_query, hidden_sem, weight_sem, small_sem, out_sem,
):
    tokens, width = hidden.shape
    rows = weight.shape[0]
    head_size = keys.shape[0]
    step = width // blocks
    core = core_ref[0]
    copies = []
    for block in range(blocks):
        columns = pl.ds(block * step, step)
        pair = [
            pltpu.make_async_copy(weight_hbm.at[:, columns], weight.at[:, columns], weight_sem.at[block]),
            pltpu.make_async_copy(hidden_hbm.at[:, columns], hidden.at[:, columns], hidden_sem.at[block]),
        ]
        for copy in pair:
            copy.start()
        copies.append(pair)
    small = [
        pltpu.make_async_copy(source, target, small_sem.at[place])
        for place, (source, target) in enumerate(
            ((keys_hbm, keys), (values_hbm, values), (grad_out_hbm, grad_out))
        )
    ]
    for copy in small:
        copy.start()
    total = jnp.zeros((tokens, rows), jnp.float32)
    for block in range(blocks):
        for copy in copies[block]:
            copy.wait()
        columns = pl.ds(block * step, step)
        total += dot_tt(hidden[:, columns], weight[:, columns])
    query = total.astype(jnp.bfloat16)
    for copy in small:
        copy.wait()
    given = grad_out[...]
    grads = jnp.concatenate(
        [
            head_grad(
                query[:, low : low + head_size], keys[...], values[...], given[:, low : low + head_size]
            )
            for low in range(0, rows, head_size)
        ],
        axis=1,
    )
    grad_query[...] = grads
    sent = [pltpu.make_async_copy(grad_query, grad_query_hbm, small_sem.at[3])]
    sent[0].start()
    half = rows // 2
    turned = jnp.where(core == 0, grads[:, half:], grads[:, :half]).T
    for block in range(blocks):
        term = dot(turned, hidden[:, pl.ds(block * step, step)])
        other[block] = term.astype(jnp.bfloat16)
        sent.append(pltpu.make_async_copy(other.at[block], other_hbm.at[block], out_sem.at[block]))
        sent[-1].start()
    for copy in sent:
        copy.wait()


def query_and_other(blocks, core, hidden_in, query_weight, keys, values, grad_out):
    tokens, width = hidden_in.shape
    rows = query_weight.shape[0]
    piece = (blocks, rows // 2, width // blocks)
    like = lambda array: pltpu.VMEM(array.shape, array.dtype)
    return pl.pallas_call(
        functools.partial(query_kernel, blocks),
        out_shape=(
            jax.ShapeDtypeStruct(piece, jnp.bfloat16),
            jax.ShapeDtypeStruct((tokens, rows), jnp.bfloat16),
        ),
        in_specs=[SCALAR] + [ANY] * 5,
        out_specs=(ANY, ANY),
        scratch_shapes=[
            like(hidden_in),
            like(query_weight),
            like(keys),
            like(values),
            like(grad_out),
            pltpu.VMEM(piece, jnp.bfloat16),
            pltpu.VMEM((tokens, rows), jnp.bfloat16),
            pltpu.SemaphoreType.DMA((blocks,)),
            pltpu.SemaphoreType.DMA((blocks,)),
            pltpu.SemaphoreType.DMA((4,)),
            pltpu.SemaphoreType.DMA((blocks,)),
        ],
        compiler_params=pltpu.CompilerParams(vmem_limit_bytes=VMEM_LIMIT),
        cost_estimate=pl.CostEstimate(
            flops=3 * tokens * width * rows,
            bytes_accessed=2 * (tokens * width + rows * width),
            transcendentals=tokens * tokens * 2,
        ),
    )(core, *(pltpu.with_memory_space_constraint(x, pltpu.HBM) for x in (hidden_in, query_weight, keys, values, grad_out)))


def own_kernel(core_ref, grad_query_hbm, hidden_hbm, own_hbm, grad_query, hidden, own, in_sem, hidden_sem, out_sem):
    blocks, half, step = own.shape
    first = pltpu.make_async_copy(grad_query_hbm, grad_query, in_sem)
    first.start()
    copies = []
    for block in range(blocks):
        columns = pl.ds(block * step, step)
        copies.append(
            pltpu.make_async_copy(hidden_hbm.at[:, columns], hidden.at[:, columns], hidden_sem.at[block])
        )
        copies[-1].start()
    first.wait()
    turned = jnp.where(core_ref[0] == 0, grad_query[:, :half], grad_query[:, half:]).T
    sent = []
    for block in range(blocks):
        copies[block].wait()
        own[block] = dot(turned, hidden[:, pl.ds(block * step, step)]).astype(jnp.bfloat16)
        sent.append(pltpu.make_async_copy(own.at[block], own_hbm.at[block], out_sem.at[block]))
        sent[-1].start()
    for copy in sent:
        copy.wait()


def own_rows(blocks, core, grad_query, hidden_in):
    tokens, width = hidden_in.shape
    rows = grad_query.shape[1]
    piece = (blocks, rows // 2, width // blocks)
    return pl.pallas_call(
        own_kernel,
        out_shape=jax.ShapeDtypeStruct(piece, jnp.bfloat16),
        in_specs=[SCALAR, ANY, ANY],
        out_specs=ANY,
        scratch_shapes=[
            pltpu.VMEM((tokens, rows), jnp.bfloat16),
            pltpu.VMEM((tokens, width), jnp.bfloat16),
            pltpu.VMEM(piece, jnp.bfloat16),
            pltpu.SemaphoreType.DMA(()),
            pltpu.SemaphoreType.DMA((blocks,)),
            pltpu.SemaphoreType.DMA((blocks,)),
        ],
        compiler_params=pltpu.CompilerParams(vmem_limit_bytes=VMEM_LIMIT),
        cost_estimate=pl.CostEstimate(
            flops=tokens * width * rows, bytes_accessed=2 * tokens * width, transcendentals=0
        ),
    )(core, grad_query, pltpu.with_memory_space_constraint(hidden_in, pltpu.HBM))


def place_kernel(core_ref, piece_hbm, out_hbm, sem):
    blocks, half, step = piece_hbm.shape
    rows = pl.ds(pl.multiple_of(core_ref[0] * half, half), half)
    copies = [
        pltpu.make_async_copy(piece_hbm.at[block], out_hbm.at[rows, pl.ds(block * step, step)], sem.at[block])
        for block in range(blocks)
    ]
    for copy in copies:
        copy.start()
    for copy in copies:
        copy.wait()


def place_kernel_on(core_ref, piece_hbm, before_hbm, out_hbm, sem):
    place_kernel(core_ref, piece_hbm, out_hbm, sem)


def place(core, piece, before=None):
    blocks, half, step = piece.shape
    return pl.pallas_call(
        place_kernel if before is None else place_kernel_on,
        out_shape=jax.ShapeDtypeStruct((2 * half, blocks * step), jnp.bfloat16),
        in_specs=[SCALAR, ANY] + [ANY] * (before is not None),
        out_specs=ANY,
        scratch_shapes=[pltpu.SemaphoreType.DMA((blocks,))],
        input_output_aliases={} if before is None else {2: 0},
        compiler_params=pltpu.CompilerParams(vmem_limit_bytes=VMEM_LIMIT),
        cost_estimate=pl.CostEstimate(flops=0, bytes_accessed=4 * half * blocks * step, transcendentals=0),
    )(core, piece, *(() if before is None else (before,)))


def swap(array, step, count):
    return lax.ppermute(array, "dp", [(i, i ^ step) for i in range(count)])


def add(left, right):
    return (left.astype(jnp.float32) + right.astype(jnp.float32)).astype(jnp.bfloat16)


def plan_of(count):
    bits = count.bit_length() - 1
    wide = min(3, bits - 1)
    group_bits = [list(range(1, wide + 1))] * 2
    later = [list(range(wide + 1, bits))] * 2
    if wide and later[1]:
        group_bits[1] = group_bits[1][:-1] + [wide + 1]
        later[1] = [wide] + later[1][1:]
    places = list(range(1 << wide))
    places = [places[half if way == 0 else -1 - half] for half in range(len(places) // 2) for way in range(2)] or places
    groups = []
    for core in range(2):
        steps = [sum((place >> at & 1) << bit for at, bit in enumerate(group_bits[core])) for place in places]
        firsts = [core + sum((rest >> at & 1) << bit for at, bit in enumerate(later[core])) for rest in range(count >> (wide + 1))]
        groups += [[first + step for step in steps] for first in firsts]
    return groups, [(1 << low, 1 << high) for low, high in zip(*later)]


def per_device(count, hidden_in, query_weight, saved_keys, saved_values, grad_out):
    groups, exchanges = plan_of(count)
    blocks = len(groups[0])
    if hidden_in.shape[1] != query_weight.shape[1]:
        hidden_in = lax.all_gather(hidden_in, "tensor", axis=1, tiled=True)
    core = (lax.axis_index("dp") & 1).astype(jnp.int32).reshape(1)
    other, grad_query = query_and_other(
        blocks, core, hidden_in, query_weight, saved_keys.T, saved_values.T, grad_out
    )
    arriving = swap(other, 1, count)
    own = own_rows(blocks, core, grad_query, hidden_in)
    chip = add(own, arriving)
    parts = lax.all_to_all(chip, "dp", 0, 0, axis_index_groups=groups)
    total = jnp.sum(parts.astype(jnp.float32), axis=0).astype(jnp.bfloat16)
    grad_query, total = lax.optimization_barrier((grad_query, total))
    input_terms = dot(grad_query, query_weight)
    grad_hidden = lax.psum_scatter(
        input_terms.astype(jnp.bfloat16), "tensor", scatter_dimension=1, tiled=True
    )
    for at, steps in enumerate(exchanges):
        arriving = lax.ppermute(total, "dp", [(i, i ^ steps[i & 1]) for i in range(count)])
        if at == 0:
            arriving, grad_hidden = lax.optimization_barrier((arriving, grad_hidden))
        total = add(total, arriving)
    copies = jnp.broadcast_to(total[None], (blocks, *total.shape))
    gathered = lax.all_to_all(copies, "dp", 0, 0, axis_index_groups=groups)
    arriving = swap(gathered, 1, count)
    grad_query_weight = place(1 - core, arriving, place(core, gathered))
    return (grad_query_weight, grad_hidden)


def solution(mesh):
    count = mesh.shape["dp"]
    placed = (
        P("dp", "tensor"),
        P("tensor", None),
        P("dp", "tensor"),
        P("dp", "tensor"),
        P("dp", "tensor"),
    )
    return jax.shard_map(
        functools.partial(per_device, count),
        mesh=mesh,
        in_specs=placed,
        out_specs=(P("tensor", None), P("dp", "tensor")),
        check_vma=False,
    )
```

```python
import functools

import jax
import jax.numpy as jnp
from jax import lax
from jax.experimental import pallas as pl
from jax.experimental.pallas import tpu as pltpu
from jax.sharding import PartitionSpec as P

LOADS = 8
VMEM_LIMIT = 40 * 1024 * 1024
ANY = pl.BlockSpec(memory_space=pl.ANY)
WHOLE = pl.BlockSpec(memory_space=pltpu.VMEM)
SCALAR = pl.BlockSpec(memory_space=pltpu.SMEM)


def dot(left, right):
    return jnp.dot(left, right, preferred_element_type=jnp.float32)


def dot_tt(left, right):
    return lax.dot_general(left, right, (((1,), (1,)), ((), ())), preferred_element_type=jnp.float32)


def head_grad(query, keys, values, grad_out):
    head_size, length = keys.shape
    score_scale = head_size ** (-0.5)
    causal_mask = lax.broadcasted_iota(jnp.int32, (length, length), 1) <= lax.broadcasted_iota(
        jnp.int32, (length, length), 0
    )
    scores = jnp.where(causal_mask, dot(query, keys) * score_scale, -1e30)
    raised = jnp.exp(scores - jnp.max(scores, axis=1, keepdims=True))
    attn_weights = raised * (1.0 / jnp.sum(raised, axis=1, keepdims=True))
    grad_prob = dot(grad_out, values)
    row_delta = jnp.sum(attn_weights * grad_prob, axis=1, keepdims=True)
    grad_score = (attn_weights * (grad_prob - row_delta) * score_scale).astype(jnp.bfloat16)
    return dot_tt(grad_score, keys).astype(jnp.bfloat16)


def heads_grad(query, keys, values, grad_out):
    size = keys.shape[0]
    heads = [slice(low, low + size) for low in range(0, query.shape[1], size)]
    grads = [head_grad(query[:, head], keys, values, grad_out[:, head]) for head in heads]
    return grads[0] if len(grads) == 1 else jnp.concatenate(grads, axis=1)


def half_of(array, second):
    half = array.shape[1] // 2
    return jnp.where(second, array[:, half:], array[:, :half])


def add_rows(grads, hidden, out):
    turned = grads.T
    step = out.shape[2]
    for block in range(out.shape[0]):
        out[block] = dot(turned, hidden[:, pl.ds(block * step, step)]).astype(out.dtype)


def query_kernel(
    core_ref, hidden_hbm, weight_hbm, keys_hbm, values_hbm, grad_out_hbm,
    other, hidden, query, grads,
    weight, keys, values, grad_out, hidden_sem, weight_sem, small_sem,
):
    tokens, width = hidden.shape
    blocks = hidden_sem.shape[0]
    step = width // blocks
    copies = []
    for block in range(blocks):
        columns = pl.ds(block * step, step)
        pair = [
            pltpu.make_async_copy(weight_hbm.at[:, columns], weight.at[:, columns], weight_sem.at[block]),
            pltpu.make_async_copy(hidden_hbm.at[:, columns], hidden.at[:, columns], hidden_sem.at[block]),
        ]
        for copy in pair:
            copy.start()
        copies.append(pair)
    pairs = ((keys_hbm, keys), (values_hbm, values), (grad_out_hbm, grad_out))
    small = [pltpu.make_async_copy(*pair, small_sem.at[at]) for at, pair in enumerate(pairs)]
    for copy in small:
        copy.start()
    total = jnp.zeros((tokens, weight.shape[0]), jnp.float32)
    for block in range(blocks):
        for copy in copies[block]:
            copy.wait()
        columns = pl.ds(block * step, step)
        total += dot_tt(hidden[:, columns], weight[:, columns])
    rounded = total.astype(jnp.bfloat16)
    query[...] = rounded
    for copy in small:
        copy.wait()
    second = core_ref[0] == 0
    found = heads_grad(half_of(rounded, second), keys[...], values[...], half_of(grad_out[...], second))
    grads[...] = found
    add_rows(found, hidden, other)


def query_and_other(blocks, core, hidden_in, query_weight, keys, values, grad_out):
    tokens, width = hidden_in.shape
    rows = query_weight.shape[0]
    like = lambda array: pltpu.VMEM(array.shape, array.dtype)
    operands = (hidden_in, query_weight, keys, values, grad_out)
    return pl.pallas_call(
        query_kernel,
        out_shape=(
            jax.ShapeDtypeStruct((blocks, rows // 2, width // blocks), jnp.bfloat16),
            jax.ShapeDtypeStruct((tokens, width), jnp.bfloat16),
            jax.ShapeDtypeStruct((tokens, rows), jnp.bfloat16),
            jax.ShapeDtypeStruct((tokens, rows // 2), jnp.bfloat16),
        ),
        in_specs=[SCALAR] + [ANY] * 5,
        out_specs=(WHOLE,) * 4,
        scratch_shapes=[
            like(query_weight),
            like(keys),
            like(values),
            like(grad_out),
            pltpu.SemaphoreType.DMA((LOADS,)),
            pltpu.SemaphoreType.DMA((LOADS,)),
            pltpu.SemaphoreType.DMA((3,)),
        ],
        compiler_params=pltpu.CompilerParams(vmem_limit_bytes=VMEM_LIMIT),
        cost_estimate=pl.CostEstimate(
            flops=3 * tokens * width * rows,
            bytes_accessed=2 * (tokens * width + rows * width),
            transcendentals=tokens * tokens,
        ),
    )(core, *(pltpu.with_memory_space_constraint(operand, pltpu.HBM) for operand in operands))


def own_kernel(core_ref, hidden, query, others, keys, values, grad_out, own, grad_query):
    second = core_ref[0] == 1
    grads = heads_grad(half_of(query[...], second), keys[...], values[...], half_of(grad_out[...], second))
    add_rows(grads, hidden, own)
    before = others[...]
    grad_query[...] = jnp.concatenate(
        [jnp.where(second, before, grads), jnp.where(second, grads, before)], axis=1
    )


def own_part(blocks, core, hidden, query, others, keys, values, grad_out):
    tokens, width = hidden.shape
    rows = query.shape[1]
    return pl.pallas_call(
        own_kernel,
        out_shape=(
            jax.ShapeDtypeStruct((blocks, rows // 2, width // blocks), jnp.bfloat16),
            jax.ShapeDtypeStruct((tokens, rows), jnp.bfloat16),
        ),
        in_specs=[SCALAR] + [WHOLE] * 6,
        out_specs=(WHOLE,) * 2,
        compiler_params=pltpu.CompilerParams(vmem_limit_bytes=24 * 1024 * 1024),
        cost_estimate=pl.CostEstimate(
            flops=tokens * width * rows, bytes_accessed=2 * tokens * width, transcendentals=tokens * tokens
        ),
    )(core, hidden, query, others, keys, values, grad_out)


def place_kernel(core_ref, piece_hbm, out_hbm, sem):
    blocks, half, step = piece_hbm.shape
    rows = pl.ds(pl.multiple_of(core_ref[0] * half, half), half)
    copies = [
        pltpu.make_async_copy(piece_hbm.at[block], out_hbm.at[rows, pl.ds(block * step, step)], sem.at[block])
        for block in range(blocks)
    ]
    for copy in copies:
        copy.start()
    for copy in copies:
        copy.wait()


def place_kernel_on(core_ref, piece_hbm, before_hbm, out_hbm, sem):
    place_kernel(core_ref, piece_hbm, out_hbm, sem)


def place(core, piece, before=None):
    blocks, half, step = piece.shape
    return pl.pallas_call(
        place_kernel if before is None else place_kernel_on,
        out_shape=jax.ShapeDtypeStruct((2 * half, blocks * step), jnp.bfloat16),
        in_specs=[SCALAR, ANY] + [ANY] * (before is not None),
        out_specs=ANY,
        scratch_shapes=[pltpu.SemaphoreType.DMA((blocks,))],
        input_output_aliases={} if before is None else {2: 0},
        compiler_params=pltpu.CompilerParams(vmem_limit_bytes=VMEM_LIMIT),
        cost_estimate=pl.CostEstimate(flops=0, bytes_accessed=4 * half * blocks * step, transcendentals=0),
    )(core, piece, *(() if before is None else (before,)))


def swap(array, step, count):
    return lax.ppermute(array, "dp", [(i, i ^ step) for i in range(count)])


def add(left, right):
    return (left.astype(jnp.float32) + right.astype(jnp.float32)).astype(jnp.bfloat16)


def per_device(count, hidden_in, query_weight, saved_keys, saved_values, grad_out):
    bits = count.bit_length() - 1
    wide = min(3, bits - 1)
    blocks = 1 << wide
    groups = [
        [high << (wide + 1) | (place ^ (high & 1) * (blocks >> 1)) << 1 | core for place in range(blocks)]
        for high in range(count >> (wide + 1))
        for core in range(2)
    ]
    if hidden_in.shape[1] != query_weight.shape[1]:
        hidden_in = lax.all_gather(hidden_in, "tensor", axis=1, tiled=True)
    core = (lax.axis_index("dp") & 1).astype(jnp.int32).reshape(1)
    keys, values = saved_keys.T, saved_values.T
    other, hidden, query, grads = query_and_other(
        blocks, core, hidden_in, query_weight, keys, values, grad_out
    )
    arriving = swap(other, 1, count)
    own, grad_query = own_part(blocks, core, hidden, query, grads, keys, values, grad_out)
    chip = add(own, arriving)
    parts = lax.all_to_all(chip, "dp", 0, 0, axis_index_groups=groups)
    total = jnp.sum(parts.astype(jnp.float32), axis=0).astype(jnp.bfloat16)
    grad_query, total = lax.optimization_barrier((grad_query, total))
    input_terms = dot(grad_query, query_weight)
    grad_hidden = lax.psum_scatter(
        input_terms.astype(jnp.bfloat16), "tensor", scatter_dimension=1, tiled=True
    )
    for bit in range(wide + 1, bits):
        arriving = swap(total, 3 << wide if bit == wide + 1 else 1 << bit, count)
        if bit == wide + 1:
            arriving, grad_hidden = lax.optimization_barrier((arriving, grad_hidden))
        total = add(total, arriving)
    copies = jnp.broadcast_to(total[None], (blocks, *total.shape))
    gathered = lax.all_to_all(copies, "dp", 0, 0, axis_index_groups=groups)
    arriving = swap(gathered, 1, count)
    grad_query_weight = place(1 - core, arriving, place(core, gathered))
    return (grad_query_weight, grad_hidden)


def solution(mesh):
    count = mesh.shape["dp"]
    placed = (
        P("dp", "tensor"),
        P("tensor", None),
        P("dp", "tensor"),
        P("dp", "tensor"),
        P("dp", "tensor"),
    )
    return jax.shard_map(
        functools.partial(per_device, count),
        mesh=mesh,
        in_specs=placed,
        out_specs=(P("tensor", None), P("dp", "tensor")),
        check_vma=False,
    )
```

```python
import functools

import jax
import jax.numpy as jnp
from jax import lax
from jax.experimental import pallas as pl
from jax.experimental.pallas import tpu as pltpu
from jax.sharding import PartitionSpec as P

LOADS = 8
VMEM_LIMIT = 40 * 1024 * 1024
ANY = pl.BlockSpec(memory_space=pl.ANY)
WHOLE = pl.BlockSpec(memory_space=pltpu.VMEM)
SCALAR = pl.BlockSpec(memory_space=pltpu.SMEM)


def dot(left, right):
    return jnp.dot(left, right, preferred_element_type=jnp.float32)


def dot_tt(left, right):
    return lax.dot_general(left, right, (((1,), (1,)), ((), ())), preferred_element_type=jnp.float32)


def head_grad(query, keys, values, grad_out):
    head_size, length = keys.shape
    score_scale = head_size ** (-0.5)
    causal_mask = lax.broadcasted_iota(jnp.int32, (length, length), 1) <= lax.broadcasted_iota(
        jnp.int32, (length, length), 0
    )
    scores = jnp.where(causal_mask, dot(query, keys) * score_scale, -1e30)
    raised = jnp.exp(scores - jnp.max(scores, axis=1, keepdims=True))
    attn_weights = raised * (1.0 / jnp.sum(raised, axis=1, keepdims=True))
    grad_prob = dot(grad_out, values)
    row_delta = jnp.sum(attn_weights * grad_prob, axis=1, keepdims=True)
    grad_score = (attn_weights * (grad_prob - row_delta) * score_scale).astype(jnp.bfloat16)
    return dot_tt(grad_score, keys).astype(jnp.bfloat16)


def heads_grad(query, keys, values, grad_out):
    size = keys.shape[0]
    heads = [slice(low, low + size) for low in range(0, query.shape[1], size)]
    grads = [head_grad(query[:, head], keys, values, grad_out[:, head]) for head in heads]
    return grads[0] if len(grads) == 1 else jnp.concatenate(grads, axis=1)


def half_of(array, second):
    half = array.shape[1] // 2
    return jnp.where(second, array[:, half:], array[:, :half])


def add_rows(grads, hidden, out):
    turned = grads.T
    step = out.shape[2]
    for block in range(out.shape[0]):
        out[block] = dot(turned, hidden[:, pl.ds(block * step, step)]).astype(out.dtype)


def query_kernel(
    core_ref, hidden_hbm, weight_hbm, keys_hbm, values_hbm, grad_out_hbm,
    other, hidden, query, grads,
    weight, keys, values, grad_out, hidden_sem, weight_sem, small_sem,
):
    tokens, width = hidden.shape
    blocks = hidden_sem.shape[0]
    step = width // blocks
    copies = []
    for block in range(blocks):
        columns = pl.ds(block * step, step)
        pair = [
            pltpu.make_async_copy(weight_hbm.at[:, columns], weight.at[:, columns], weight_sem.at[block]),
            pltpu.make_async_copy(hidden_hbm.at[:, columns], hidden.at[:, columns], hidden_sem.at[block]),
        ]
        for copy in pair:
            copy.start()
        copies.append(pair)
    pairs = ((keys_hbm, keys), (values_hbm, values), (grad_out_hbm, grad_out))
    small = [pltpu.make_async_copy(*pair, small_sem.at[at]) for at, pair in enumerate(pairs)]
    for copy in small:
        copy.start()
    total = jnp.zeros((tokens, weight.shape[0]), jnp.float32)
    for block in range(blocks):
        for copy in copies[block]:
            copy.wait()
        columns = pl.ds(block * step, step)
        total += dot_tt(hidden[:, columns], weight[:, columns])
    rounded = total.astype(jnp.bfloat16)
    query[...] = rounded
    for copy in small:
        copy.wait()
    second = core_ref[0] == 0
    found = heads_grad(half_of(rounded, second), keys[...], values[...], half_of(grad_out[...], second))
    grads[...] = found
    add_rows(found, hidden, other)


def query_and_other(blocks, core, hidden_in, query_weight, keys, values, grad_out):
    tokens, width = hidden_in.shape
    rows = query_weight.shape[0]
    like = lambda array: pltpu.VMEM(array.shape, array.dtype)
    operands = (hidden_in, query_weight, keys, values, grad_out)
    return pl.pallas_call(
        query_kernel,
        out_shape=(
            jax.ShapeDtypeStruct((blocks, rows // 2, width // blocks), jnp.bfloat16),
            jax.ShapeDtypeStruct((tokens, width), jnp.bfloat16),
            jax.ShapeDtypeStruct((tokens, rows), jnp.bfloat16),
            jax.ShapeDtypeStruct((tokens, rows // 2), jnp.bfloat16),
        ),
        in_specs=[SCALAR] + [ANY] * 5,
        out_specs=(WHOLE,) * 4,
        scratch_shapes=[
            like(query_weight),
            like(keys),
            like(values),
            like(grad_out),
            pltpu.SemaphoreType.DMA((LOADS,)),
            pltpu.SemaphoreType.DMA((LOADS,)),
            pltpu.SemaphoreType.DMA((3,)),
        ],
        compiler_params=pltpu.CompilerParams(vmem_limit_bytes=VMEM_LIMIT),
        cost_estimate=pl.CostEstimate(
            flops=3 * tokens * width * rows,
            bytes_accessed=2 * (tokens * width + rows * width),
            transcendentals=tokens * tokens,
        ),
    )(core, *(pltpu.with_memory_space_constraint(operand, pltpu.HBM) for operand in operands))


def own_kernel(core_ref, hidden, query, others, keys, values, grad_out, own, grad_query):
    second = core_ref[0] == 1
    grads = heads_grad(half_of(query[...], second), keys[...], values[...], half_of(grad_out[...], second))
    add_rows(grads, hidden, own)
    before = others[...]
    grad_query[...] = jnp.concatenate(
        [jnp.where(second, before, grads), jnp.where(second, grads, before)], axis=1
    )


def own_part(blocks, core, hidden, query, others, keys, values, grad_out):
    tokens, width = hidden.shape
    rows = query.shape[1]
    return pl.pallas_call(
        own_kernel,
        out_shape=(
            jax.ShapeDtypeStruct((blocks, rows // 2, width // blocks), jnp.bfloat16),
            jax.ShapeDtypeStruct((tokens, rows), jnp.bfloat16),
        ),
        in_specs=[SCALAR] + [WHOLE] * 6,
        out_specs=(WHOLE,) * 2,
        compiler_params=pltpu.CompilerParams(vmem_limit_bytes=24 * 1024 * 1024),
        cost_estimate=pl.CostEstimate(
            flops=tokens * width * rows, bytes_accessed=2 * tokens * width, transcendentals=tokens * tokens
        ),
    )(core, hidden, query, others, keys, values, grad_out)


def hidden_kernel(core_ref, turn_ref, grad_query, weight_hbm, *refs):
    out_hbm, weight, found, weight_sem, out_sem = refs[-5:]

    @pl.when(core_ref[0] == turn_ref[0])
    def _():
        blocks, _, step = found.shape
        copies = []
        for block in range(blocks):
            columns = pl.ds(block * step, step)
            copies.append(
                pltpu.make_async_copy(weight_hbm.at[:, columns], weight.at[:, columns], weight_sem.at[block])
            )
            copies[-1].start()
        grads = grad_query[...]
        sent = []
        for block in range(blocks):
            columns = pl.ds(block * step, step)
            copies[block].wait()
            found[block] = dot(grads, weight[:, columns]).astype(found.dtype)
            sent.append(pltpu.make_async_copy(found.at[block], out_hbm.at[:, columns], out_sem.at[block]))
            sent[-1].start()
        for copy in sent:
            copy.wait()


def hidden_part(core, turn, grad_query, query_weight, before=None):
    tokens, rows = grad_query.shape
    width = query_weight.shape[1]
    given = () if before is None else (before,)
    return pl.pallas_call(
        hidden_kernel,
        out_shape=jax.ShapeDtypeStruct((tokens, width), jnp.bfloat16),
        in_specs=[SCALAR, SCALAR, WHOLE, ANY] + [ANY] * len(given),
        out_specs=ANY,
        scratch_shapes=[
            pltpu.VMEM((rows, width), jnp.bfloat16),
            pltpu.VMEM((LOADS, tokens, width // LOADS), jnp.bfloat16),
            pltpu.SemaphoreType.DMA((LOADS,)),
            pltpu.SemaphoreType.DMA((LOADS,)),
        ],
        input_output_aliases={4: 0} if given else {},
        compiler_params=pltpu.CompilerParams(vmem_limit_bytes=24 * 1024 * 1024),
        cost_estimate=pl.CostEstimate(
            flops=2 * tokens * width * rows, bytes_accessed=2 * width * (tokens + rows), transcendentals=0
        ),
    )(core, jnp.full((1,), turn, jnp.int32), grad_query, pltpu.with_memory_space_constraint(query_weight, pltpu.HBM), *given)


def place_kernel(core_ref, piece_hbm, out_hbm, sem):
    blocks, half, step = piece_hbm.shape
    rows = pl.ds(pl.multiple_of(core_ref[0] * half, half), half)
    copies = [
        pltpu.make_async_copy(piece_hbm.at[block], out_hbm.at[rows, pl.ds(block * step, step)], sem.at[block])
        for block in range(blocks)
    ]
    for copy in copies:
        copy.start()
    for copy in copies:
        copy.wait()


def place_kernel_on(core_ref, piece_hbm, before_hbm, out_hbm, sem):
    place_kernel(core_ref, piece_hbm, out_hbm, sem)


def place(core, piece, before=None):
    blocks, half, step = piece.shape
    return pl.pallas_call(
        place_kernel if before is None else place_kernel_on,
        out_shape=jax.ShapeDtypeStruct((2 * half, blocks * step), jnp.bfloat16),
        in_specs=[SCALAR, ANY] + [ANY] * (before is not None),
        out_specs=ANY,
        scratch_shapes=[pltpu.SemaphoreType.DMA((blocks,))],
        input_output_aliases={} if before is None else {2: 0},
        compiler_params=pltpu.CompilerParams(vmem_limit_bytes=VMEM_LIMIT),
        cost_estimate=pl.CostEstimate(flops=0, bytes_accessed=4 * half * blocks * step, transcendentals=0),
    )(core, piece, *(() if before is None else (before,)))


def swap(array, step, count):
    return lax.ppermute(array, "dp", [(i, i ^ step) for i in range(count)])


def add(left, right):
    return (left.astype(jnp.float32) + right.astype(jnp.float32)).astype(jnp.bfloat16)


def per_device(count, hidden_in, query_weight, saved_keys, saved_values, grad_out):
    bits = count.bit_length() - 1
    wide = min(3, bits - 1)
    blocks = 1 << wide
    groups = [
        [high << (wide + 1) | (place ^ (high & 1) * (blocks >> 1)) << 1 | core for place in range(blocks)]
        for high in range(count >> (wide + 1))
        for core in range(2)
    ]
    given_width = hidden_in.shape[1]
    if given_width != query_weight.shape[1]:
        hidden_in = lax.all_gather(hidden_in, "tensor", axis=1, tiled=True)
    core = (lax.axis_index("dp") & 1).astype(jnp.int32).reshape(1)
    keys, values = saved_keys.T, saved_values.T
    other, hidden, query, grads = query_and_other(
        blocks, core, hidden_in, query_weight, keys, values, grad_out
    )
    arriving = swap(other, 1, count)
    own, grad_query = own_part(blocks, core, hidden, query, grads, keys, values, grad_out)
    chip = add(own, arriving)
    input_terms = hidden_part(core, 0, grad_query, query_weight)
    chip, input_terms = lax.optimization_barrier((chip, input_terms))
    parts = lax.all_to_all(chip, "dp", 0, 0, axis_index_groups=groups)
    total = jnp.sum(parts.astype(jnp.float32), axis=0).astype(jnp.bfloat16)
    input_terms, total = lax.optimization_barrier((input_terms, total))
    input_terms = hidden_part(core, 1, grad_query, query_weight, input_terms)
    for bit in range(wide + 1, bits):
        arriving = swap(total, 3 << wide if bit == wide + 1 else 1 << bit, count)
        if bit == wide + 1:
            arriving, input_terms = lax.optimization_barrier((arriving, input_terms))
        total = add(total, arriving)
    copies = jnp.broadcast_to(total[None], (blocks, *total.shape))
    gathered = lax.all_to_all(copies, "dp", 0, 0, axis_index_groups=groups)
    arriving = swap(gathered, 1, count)
    grad_query_weight = place(1 - core, arriving, place(core, gathered))
    if input_terms.shape[1] == given_width:
        grad_hidden = input_terms
    else:
        grad_hidden = lax.psum_scatter(input_terms, "tensor", scatter_dimension=1, tiled=True)
    return (grad_query_weight, grad_hidden)


def solution(mesh):
    count = mesh.shape["dp"]
    placed = (
        P("dp", "tensor"),
        P("tensor", None),
        P("dp", "tensor"),
        P("dp", "tensor"),
        P("dp", "tensor"),
    )
    return jax.shard_map(
        functools.partial(per_device, count),
        mesh=mesh,
        in_specs=placed,
        out_specs=(P("tensor", None), P("dp", "tensor")),
        check_vma=False,
    )
```

```python
import functools

import jax
import jax.numpy as jnp
from jax import lax
from jax.experimental import pallas as pl
from jax.experimental.pallas import tpu as pltpu
from jax.sharding import PartitionSpec as P

LOADS = 8
VMEM_LIMIT = 40 * 1024 * 1024
ANY = pl.BlockSpec(memory_space=pl.ANY)
WHOLE = pl.BlockSpec(memory_space=pltpu.VMEM)


def own_core():
    return lax.axis_index("dp") & 1


def dot(left, right):
    return jnp.dot(left, right, preferred_element_type=jnp.float32)


def dot_tt(left, right):
    return lax.dot_general(left, right, (((1,), (1,)), ((), ())), preferred_element_type=jnp.float32)


def head_grad(query, keys, values, grad_out):
    head_size, length = keys.shape
    score_scale = head_size ** (-0.5)
    causal_mask = lax.broadcasted_iota(jnp.int32, (length, length), 1) <= lax.broadcasted_iota(
        jnp.int32, (length, length), 0
    )
    scores = jnp.where(causal_mask, dot(query, keys) * score_scale, -1e30)
    raised = jnp.exp(scores - jnp.max(scores, axis=1, keepdims=True))
    attn_weights = raised * (1.0 / jnp.sum(raised, axis=1, keepdims=True))
    grad_prob = dot(grad_out, values)
    row_delta = jnp.sum(attn_weights * grad_prob, axis=1, keepdims=True)
    grad_score = (attn_weights * (grad_prob - row_delta) * score_scale).astype(jnp.bfloat16)
    return dot_tt(grad_score, keys).astype(jnp.bfloat16)


def heads_grad(query, keys, values, grad_out):
    size = keys.shape[0]
    heads = [slice(low, low + size) for low in range(0, query.shape[1], size)]
    grads = [head_grad(query[:, head], keys, values, grad_out[:, head]) for head in heads]
    return grads[0] if len(grads) == 1 else jnp.concatenate(grads, axis=1)


def half_of(array, second):
    half = array.shape[1] // 2
    return jnp.where(second, array[:, half:], array[:, :half])


def add_rows(grads, hidden, out):
    turned = grads.T
    step = out.shape[2]
    for block in range(out.shape[0]):
        out[block] = dot(turned, hidden[:, pl.ds(block * step, step)]).astype(out.dtype)


def query_kernel(
    hidden_hbm, weight_hbm, keys_hbm, values_hbm, grad_out_hbm,
    other, hidden, query, grads,
    weight, keys, values, grad_out, hidden_sem, weight_sem, small_sem,
):
    tokens, width = hidden.shape
    blocks = hidden_sem.shape[0]
    step = width // blocks
    copies = []
    for block in range(blocks):
        columns = pl.ds(block * step, step)
        pair = [
            pltpu.make_async_copy(weight_hbm.at[:, columns], weight.at[:, columns], weight_sem.at[block]),
            pltpu.make_async_copy(hidden_hbm.at[:, columns], hidden.at[:, columns], hidden_sem.at[block]),
        ]
        for copy in pair:
            copy.start()
        copies.append(pair)
    pairs = ((keys_hbm, keys), (values_hbm, values), (grad_out_hbm, grad_out))
    small = [pltpu.make_async_copy(*pair, small_sem.at[at]) for at, pair in enumerate(pairs)]
    for copy in small:
        copy.start()
    total = jnp.zeros((tokens, weight.shape[0]), jnp.float32)
    for block in range(blocks):
        for copy in copies[block]:
            copy.wait()
        columns = pl.ds(block * step, step)
        total += dot_tt(hidden[:, columns], weight[:, columns])
    rounded = total.astype(jnp.bfloat16)
    query[...] = rounded
    for copy in small:
        copy.wait()
    second = own_core() == 0
    found = heads_grad(half_of(rounded, second), keys[...], values[...], half_of(grad_out[...], second))
    grads[...] = found
    add_rows(found, hidden, other)


def query_and_other(blocks, hidden_in, query_weight, keys, values, grad_out):
    tokens, width = hidden_in.shape
    rows = query_weight.shape[0]
    like = lambda array: pltpu.VMEM(array.shape, array.dtype)
    operands = (hidden_in, query_weight, keys, values, grad_out)
    return pl.pallas_call(
        query_kernel,
        out_shape=(
            jax.ShapeDtypeStruct((blocks, rows // 2, width // blocks), jnp.bfloat16),
            jax.ShapeDtypeStruct((tokens, width), jnp.bfloat16),
            jax.ShapeDtypeStruct((tokens, rows), jnp.bfloat16),
            jax.ShapeDtypeStruct((tokens, rows // 2), jnp.bfloat16),
        ),
        in_specs=[ANY] * 5,
        out_specs=(WHOLE,) * 4,
        scratch_shapes=[
            like(query_weight),
            like(keys),
            like(values),
            like(grad_out),
            pltpu.SemaphoreType.DMA((LOADS,)),
            pltpu.SemaphoreType.DMA((LOADS,)),
            pltpu.SemaphoreType.DMA((3,)),
        ],
        compiler_params=pltpu.CompilerParams(vmem_limit_bytes=VMEM_LIMIT),
        cost_estimate=pl.CostEstimate(
            flops=3 * tokens * width * rows,
            bytes_accessed=2 * (tokens * width + rows * width),
            transcendentals=tokens * tokens,
        ),
    )(*(pltpu.with_memory_space_constraint(operand, pltpu.HBM) for operand in operands))


def own_kernel(hidden, query, others, keys, values, grad_out, own, grad_query):
    second = own_core() == 1
    grads = heads_grad(half_of(query[...], second), keys[...], values[...], half_of(grad_out[...], second))
    add_rows(grads, hidden, own)
    before = others[...]
    grad_query[...] = jnp.concatenate(
        [jnp.where(second, before, grads), jnp.where(second, grads, before)], axis=1
    )


def own_part(blocks, hidden, query, others, keys, values, grad_out):
    tokens, width = hidden.shape
    rows = query.shape[1]
    return pl.pallas_call(
        own_kernel,
        out_shape=(
            jax.ShapeDtypeStruct((blocks, rows // 2, width // blocks), jnp.bfloat16),
            jax.ShapeDtypeStruct((tokens, rows), jnp.bfloat16),
        ),
        in_specs=[WHOLE] * 6,
        out_specs=(WHOLE,) * 2,
        compiler_params=pltpu.CompilerParams(vmem_limit_bytes=24 * 1024 * 1024),
        cost_estimate=pl.CostEstimate(
            flops=tokens * width * rows, bytes_accessed=2 * tokens * width, transcendentals=tokens * tokens
        ),
    )(hidden, query, others, keys, values, grad_out)


def hidden_kernel(turn, grad_query, weight_hbm, *refs):
    out_hbm, weight, found, weight_sem, out_sem = refs[-5:]

    @pl.when(own_core() == turn)
    def _():
        blocks, _, step = found.shape
        copies = []
        for block in range(blocks):
            columns = pl.ds(block * step, step)
            copies.append(
                pltpu.make_async_copy(weight_hbm.at[:, columns], weight.at[:, columns], weight_sem.at[block])
            )
            copies[-1].start()
        grads = grad_query[...]
        sent = []
        for block in range(blocks):
            columns = pl.ds(block * step, step)
            copies[block].wait()
            found[block] = dot(grads, weight[:, columns]).astype(found.dtype)
            sent.append(pltpu.make_async_copy(found.at[block], out_hbm.at[:, columns], out_sem.at[block]))
            sent[-1].start()
        for copy in sent:
            copy.wait()


def hidden_part(turn, grad_query, query_weight, before=None):
    tokens, rows = grad_query.shape
    width = query_weight.shape[1]
    given = () if before is None else (before,)
    return pl.pallas_call(
        functools.partial(hidden_kernel, turn),
        out_shape=jax.ShapeDtypeStruct((tokens, width), jnp.bfloat16),
        in_specs=[WHOLE, ANY] + [ANY] * len(given),
        out_specs=ANY,
        scratch_shapes=[
            pltpu.VMEM((rows, width), jnp.bfloat16),
            pltpu.VMEM((LOADS, tokens, width // LOADS), jnp.bfloat16),
            pltpu.SemaphoreType.DMA((LOADS,)),
            pltpu.SemaphoreType.DMA((LOADS,)),
        ],
        input_output_aliases={2: 0} if given else {},
        compiler_params=pltpu.CompilerParams(vmem_limit_bytes=24 * 1024 * 1024),
        cost_estimate=pl.CostEstimate(
            flops=2 * tokens * width * rows, bytes_accessed=2 * width * (tokens + rows), transcendentals=0
        ),
    )(grad_query, pltpu.with_memory_space_constraint(query_weight, pltpu.HBM), *given)


def place_kernel(turned, piece_hbm, *refs):
    out_hbm, sem = refs[-2:]
    blocks, half, step = piece_hbm.shape
    rows = pl.ds(pl.multiple_of((own_core() ^ turned) * half, half), half)
    copies = [
        pltpu.make_async_copy(piece_hbm.at[block], out_hbm.at[rows, pl.ds(block * step, step)], sem.at[block])
        for block in range(blocks)
    ]
    for copy in copies:
        copy.start()
    for copy in copies:
        copy.wait()


def place(turned, piece, before=None):
    blocks, half, step = piece.shape
    return pl.pallas_call(
        functools.partial(place_kernel, turned),
        out_shape=jax.ShapeDtypeStruct((2 * half, blocks * step), jnp.bfloat16),
        in_specs=[ANY] + [ANY] * (before is not None),
        out_specs=ANY,
        scratch_shapes=[pltpu.SemaphoreType.DMA((blocks,))],
        input_output_aliases={} if before is None else {1: 0},
        compiler_params=pltpu.CompilerParams(vmem_limit_bytes=VMEM_LIMIT),
        cost_estimate=pl.CostEstimate(flops=0, bytes_accessed=4 * half * blocks * step, transcendentals=0),
    )(piece, *(() if before is None else (before,)))


def swap(array, step, count):
    return lax.ppermute(array, "dp", [(i, i ^ step) for i in range(count)])


def add(left, right):
    return (left.astype(jnp.float32) + right.astype(jnp.float32)).astype(jnp.bfloat16)


def per_device(count, hidden_in, query_weight, saved_keys, saved_values, grad_out):
    bits = count.bit_length() - 1
    wide = min(3, bits - 1)
    blocks = 1 << wide
    groups = [
        [high << (wide + 1) | (place ^ (high & 1) * (blocks >> 1)) << 1 | core for place in range(blocks)]
        for high in range(count >> (wide + 1))
        for core in range(2)
    ]
    given_width = hidden_in.shape[1]
    if given_width != query_weight.shape[1]:
        hidden_in = lax.all_gather(hidden_in, "tensor", axis=1, tiled=True)
    keys, values = saved_keys.T, saved_values.T
    other, hidden, query, grads = query_and_other(
        blocks, hidden_in, query_weight, keys, values, grad_out
    )
    arriving = swap(other, 1, count)
    own, grad_query = own_part(blocks, hidden, query, grads, keys, values, grad_out)
    chip = add(own, arriving)
    input_terms = hidden_part(0, grad_query, query_weight)
    chip, input_terms = lax.optimization_barrier((chip, input_terms))
    parts = lax.all_to_all(chip, "dp", 0, 0, axis_index_groups=groups)
    total = jnp.sum(parts.astype(jnp.float32), axis=0).astype(jnp.bfloat16)
    for bit in range(wide + 1, bits):
        arriving = swap(total, 3 << wide if bit == wide + 1 else 1 << bit, count)
        total = add(total, arriving)
    copies = jnp.broadcast_to(total[None], (blocks, *total.shape))
    gathered = lax.all_to_all(copies, "dp", 0, 0, axis_index_groups=groups)
    input_terms, gathered = lax.optimization_barrier((input_terms, gathered))
    input_terms = hidden_part(1, grad_query, query_weight, input_terms)
    input_terms, gathered = lax.optimization_barrier((input_terms, gathered))
    arriving = swap(gathered, 1, count)
    grad_query_weight = place(1, arriving, place(0, gathered))
    if input_terms.shape[1] == given_width:
        grad_hidden = input_terms
    else:
        grad_hidden = lax.psum_scatter(input_terms, "tensor", scatter_dimension=1, tiled=True)
    return (grad_query_weight, grad_hidden)


def solution(mesh):
    count = mesh.shape["dp"]
    placed = (
        P("dp", "tensor"),
        P("tensor", None),
        P("dp", "tensor"),
        P("dp", "tensor"),
        P("dp", "tensor"),
    )
    return jax.shard_map(
        functools.partial(per_device, count),
        mesh=mesh,
        in_specs=placed,
        out_specs=(P("tensor", None), P("dp", "tensor")),
        check_vma=False,
    )
```

```python
import functools

import jax
import jax.numpy as jnp
from jax import lax
from jax.experimental import pallas as pl
from jax.experimental.pallas import tpu as pltpu
from jax.sharding import PartitionSpec as P

LOADS = 4
VMEM_LIMIT = 40 * 1024 * 1024
ANY = pl.BlockSpec(memory_space=pl.ANY)
WHOLE = pl.BlockSpec(memory_space=pltpu.VMEM)


def own_core():
    return lax.axis_index("dp") & 1


def dot(left, right):
    return jnp.dot(left, right, preferred_element_type=jnp.float32)


def dot_tt(left, right):
    return lax.dot_general(left, right, (((1,), (1,)), ((), ())), preferred_element_type=jnp.float32)


def head_grad(query, keys, values, grad_out):
    head_size, length = keys.shape
    score_scale = head_size ** (-0.5)
    causal_mask = lax.broadcasted_iota(jnp.int32, (length, length), 1) <= lax.broadcasted_iota(
        jnp.int32, (length, length), 0
    )
    scores = jnp.where(causal_mask, dot(query, keys) * score_scale, -1e30)
    raised = jnp.exp(scores - jnp.max(scores, axis=1, keepdims=True))
    attn_weights = raised * (1.0 / jnp.sum(raised, axis=1, keepdims=True))
    grad_prob = dot(grad_out, values)
    row_delta = jnp.sum(attn_weights * grad_prob, axis=1, keepdims=True)
    grad_score = (attn_weights * (grad_prob - row_delta) * score_scale).astype(jnp.bfloat16)
    return dot_tt(grad_score, keys).astype(jnp.bfloat16)


def heads_grad(query, keys, values, grad_out):
    size = keys.shape[0]
    heads = [slice(low, low + size) for low in range(0, query.shape[1], size)]
    grads = [head_grad(query[:, head], keys, values, grad_out[:, head]) for head in heads]
    return grads[0] if len(grads) == 1 else jnp.concatenate(grads, axis=1)


def half_of(array, second):
    half = array.shape[1] // 2
    return jnp.where(second, array[:, half:], array[:, :half])


def add_rows(grads, hidden, out):
    turned = grads.T
    step = out.shape[2]
    for block in range(out.shape[0]):
        out[block] = dot(turned, hidden[:, pl.ds(block * step, step)]).astype(out.dtype)


def query_kernel(
    hidden_hbm, weight_hbm, keys_hbm, values_hbm, grad_out_hbm,
    other, hidden, weight, query, grads,
    turned, keys, values, grad_out, hidden_sem, weight_sem, small_sem,
):
    tokens, width = hidden.shape
    step = width // LOADS
    chunks = [pl.ds(at * step, step) for at in range(LOADS)]
    weights = [
        pltpu.make_async_copy(weight_hbm.at[:, columns], weight.at[:, columns], weight_sem.at[at])
        for at, columns in enumerate(chunks)
    ]
    hiddens = [
        pltpu.make_async_copy(hidden_hbm.at[:, columns], hidden.at[:, columns], hidden_sem.at[at])
        for at, columns in enumerate(chunks)
    ]
    pairs = ((keys_hbm, keys), (values_hbm, values), (grad_out_hbm, grad_out))
    small = [pltpu.make_async_copy(*pair, small_sem.at[at]) for at, pair in enumerate(pairs)]
    for copy in weights + hiddens + small:
        copy.start()
    total = jnp.zeros((tokens, weight.shape[0]), jnp.float32)
    for at, columns in enumerate(chunks):
        weights[at].wait()
        turned[columns, :] = weight[:, columns].T
        hiddens[at].wait()
        total += dot(hidden[:, columns], turned[columns, :])
    rounded = total.astype(jnp.bfloat16)
    query[...] = rounded
    for copy in small:
        copy.wait()
    second = own_core() == 0
    found = heads_grad(half_of(rounded, second), keys[...], values[...], half_of(grad_out[...], second))
    grads[...] = found
    add_rows(found, hidden, other)


def query_and_other(blocks, hidden_in, query_weight, keys, values, grad_out):
    tokens, width = hidden_in.shape
    rows = query_weight.shape[0]
    like = lambda array: pltpu.VMEM(array.shape, array.dtype)
    operands = (hidden_in, query_weight, keys, values, grad_out)
    return pl.pallas_call(
        query_kernel,
        out_shape=(
            jax.ShapeDtypeStruct((blocks, rows // 2, width // blocks), jnp.bfloat16),
            jax.ShapeDtypeStruct((tokens, width), jnp.bfloat16),
            jax.ShapeDtypeStruct((rows, width), jnp.bfloat16),
            jax.ShapeDtypeStruct((tokens, rows), jnp.bfloat16),
            jax.ShapeDtypeStruct((tokens, rows // 2), jnp.bfloat16),
        ),
        in_specs=[ANY] * 5,
        out_specs=(WHOLE,) * 5,
        scratch_shapes=[
            pltpu.VMEM((width, rows), jnp.bfloat16),
            like(keys),
            like(values),
            like(grad_out),
            pltpu.SemaphoreType.DMA((LOADS,)),
            pltpu.SemaphoreType.DMA((LOADS,)),
            pltpu.SemaphoreType.DMA((3,)),
        ],
        compiler_params=pltpu.CompilerParams(vmem_limit_bytes=VMEM_LIMIT),
        cost_estimate=pl.CostEstimate(
            flops=3 * tokens * width * rows,
            bytes_accessed=2 * (tokens * width + rows * width),
            transcendentals=tokens * tokens,
        ),
    )(*(pltpu.with_memory_space_constraint(operand, pltpu.HBM) for operand in operands))


def own_kernel(hidden, query, others, keys, values, grad_out, own, grad_query):
    second = own_core() == 1
    grads = heads_grad(half_of(query[...], second), keys[...], values[...], half_of(grad_out[...], second))
    add_rows(grads, hidden, own)
    before = others[...]
    grad_query[...] = jnp.concatenate(
        [jnp.where(second, before, grads), jnp.where(second, grads, before)], axis=1
    )


def own_part(blocks, hidden, query, others, keys, values, grad_out):
    tokens, width = hidden.shape
    rows = query.shape[1]
    return pl.pallas_call(
        own_kernel,
        out_shape=(
            jax.ShapeDtypeStruct((blocks, rows // 2, width // blocks), jnp.bfloat16),
            jax.ShapeDtypeStruct((tokens, rows), jnp.bfloat16),
        ),
        in_specs=[WHOLE] * 6,
        out_specs=(WHOLE,) * 2,
        compiler_params=pltpu.CompilerParams(vmem_limit_bytes=24 * 1024 * 1024),
        cost_estimate=pl.CostEstimate(
            flops=tokens * width * rows, bytes_accessed=2 * tokens * width, transcendentals=tokens * tokens
        ),
    )(hidden, query, others, keys, values, grad_out)


def hidden_kernel(turn, grad_query, weight, *refs):
    out_hbm, found, sem = refs[-3:]

    @pl.when(own_core() == turn)
    def _():
        pieces, _, step = found.shape
        grads = grad_query[...]
        sent = []
        for piece in range(pieces):
            columns = pl.ds(piece * step, step)
            found[piece] = dot(grads, weight[:, columns]).astype(found.dtype)
            sent.append(pltpu.make_async_copy(found.at[piece], out_hbm.at[:, columns], sem.at[piece]))
            sent[-1].start()
        for copy in sent:
            copy.wait()


def hidden_part(turn, grad_query, weight, before=None):
    tokens, rows = grad_query.shape
    width = weight.shape[1]
    given = () if before is None else (before,)
    return pl.pallas_call(
        functools.partial(hidden_kernel, turn),
        out_shape=jax.ShapeDtypeStruct((tokens, width), jnp.bfloat16),
        in_specs=[WHOLE, WHOLE] + [ANY] * len(given),
        out_specs=ANY,
        scratch_shapes=[
            pltpu.VMEM((LOADS, tokens, width // LOADS), jnp.bfloat16),
            pltpu.SemaphoreType.DMA((LOADS,)),
        ],
        input_output_aliases={2: 0} if given else {},
        compiler_params=pltpu.CompilerParams(vmem_limit_bytes=24 * 1024 * 1024),
        cost_estimate=pl.CostEstimate(
            flops=2 * tokens * width * rows, bytes_accessed=2 * width * (tokens + rows), transcendentals=0
        ),
    )(grad_query, weight, *given)


def place_kernel(turned, piece_hbm, *refs):
    out_hbm, sem = refs[-2:]
    blocks, half, step = piece_hbm.shape
    rows = pl.ds(pl.multiple_of((own_core() ^ turned) * half, half), half)
    copies = [
        pltpu.make_async_copy(piece_hbm.at[block], out_hbm.at[rows, pl.ds(block * step, step)], sem.at[block])
        for block in range(blocks)
    ]
    for copy in copies:
        copy.start()
    for copy in copies:
        copy.wait()


def place(turned, piece, before=None):
    blocks, half, step = piece.shape
    return pl.pallas_call(
        functools.partial(place_kernel, turned),
        out_shape=jax.ShapeDtypeStruct((2 * half, blocks * step), jnp.bfloat16),
        in_specs=[ANY] + [ANY] * (before is not None),
        out_specs=ANY,
        scratch_shapes=[pltpu.SemaphoreType.DMA((blocks,))],
        input_output_aliases={} if before is None else {1: 0},
        compiler_params=pltpu.CompilerParams(vmem_limit_bytes=VMEM_LIMIT),
        cost_estimate=pl.CostEstimate(flops=0, bytes_accessed=4 * half * blocks * step, transcendentals=0),
    )(piece, *(() if before is None else (before,)))


def swap(array, step, count):
    return lax.ppermute(array, "dp", [(i, i ^ step) for i in range(count)])


def add(left, right):
    return (left.astype(jnp.float32) + right.astype(jnp.float32)).astype(jnp.bfloat16)


def per_device(count, hidden_in, query_weight, saved_keys, saved_values, grad_out):
    bits = count.bit_length() - 1
    wide = min(3, bits - 1)
    blocks = 1 << wide
    groups = [
        [high << (wide + 1) | (place ^ (high & 1) * (blocks >> 1)) << 1 | core for place in range(blocks)]
        for high in range(count >> (wide + 1))
        for core in range(2)
    ]
    given_width = hidden_in.shape[1]
    if given_width != query_weight.shape[1]:
        hidden_in = lax.all_gather(hidden_in, "tensor", axis=1, tiled=True)
    keys, values = saved_keys.T, saved_values.T
    other, hidden, weight, query, grads = query_and_other(
        blocks, hidden_in, query_weight, keys, values, grad_out
    )
    arriving = swap(other, 1, count)
    own, grad_query = own_part(blocks, hidden, query, grads, keys, values, grad_out)
    chip = add(own, arriving)
    input_terms = hidden_part(0, grad_query, weight)
    chip, input_terms = lax.optimization_barrier((chip, input_terms))
    parts = lax.all_to_all(chip, "dp", 0, 0, axis_index_groups=groups)
    total = jnp.sum(parts.astype(jnp.float32), axis=0).astype(jnp.bfloat16)
    input_terms, total = lax.optimization_barrier((input_terms, total))
    input_terms = hidden_part(1, grad_query, weight, input_terms)
    for bit in range(wide + 1, bits):
        arriving = swap(total, 3 << wide if bit == wide + 1 else 1 << bit, count)
        if bit == wide + 1:
            arriving, input_terms = lax.optimization_barrier((arriving, input_terms))
        total = add(total, arriving)
    copies = jnp.broadcast_to(total[None], (blocks, *total.shape))
    gathered = lax.all_to_all(copies, "dp", 0, 0, axis_index_groups=groups)
    arriving = swap(gathered, 1, count)
    grad_query_weight = place(1, arriving, place(0, gathered))
    if input_terms.shape[1] == given_width:
        grad_hidden = input_terms
    else:
        grad_hidden = lax.psum_scatter(input_terms, "tensor", scatter_dimension=1, tiled=True)
    return (grad_query_weight, grad_hidden)


def solution(mesh):
    count = mesh.shape["dp"]
    placed = (
        P("dp", "tensor"),
        P("tensor", None),
        P("dp", "tensor"),
        P("dp", "tensor"),
        P("dp", "tensor"),
    )
    return jax.shard_map(
        functools.partial(per_device, count),
        mesh=mesh,
        in_specs=placed,
        out_specs=(P("tensor", None), P("dp", "tensor")),
        check_vma=False,
    )
```

```python
import functools

import jax
import jax.numpy as jnp
from jax import lax
from jax.experimental import pallas as pl
from jax.experimental.pallas import tpu as pltpu
from jax.sharding import PartitionSpec as P

LOADS = 4
LAST = 2
VMEM_LIMIT = 40 * 1024 * 1024
ANY = pl.BlockSpec(memory_space=pl.ANY)
WHOLE = pl.BlockSpec(memory_space=pltpu.VMEM)


def own_core():
    return lax.axis_index("dp") & 1


def own_place(blocks):
    index = lax.axis_index("dp") >> 1
    return (index & (blocks - 1)) ^ ((index >> (blocks.bit_length() - 1) & 1) * (blocks >> 1))


def dot(left, right):
    return jnp.dot(left, right, preferred_element_type=jnp.float32)


def dot_tt(left, right):
    return lax.dot_general(left, right, (((1,), (1,)), ((), ())), preferred_element_type=jnp.float32)


def head_grad(query, keys, values, grad_out):
    head_size, length = keys.shape
    score_scale = head_size ** (-0.5)
    causal_mask = lax.broadcasted_iota(jnp.int32, (length, length), 1) <= lax.broadcasted_iota(
        jnp.int32, (length, length), 0
    )
    scores = jnp.where(causal_mask, dot(query, keys) * score_scale, -1e30)
    raised = jnp.exp(scores - jnp.max(scores, axis=1, keepdims=True))
    attn_weights = raised * (1.0 / jnp.sum(raised, axis=1, keepdims=True))
    grad_prob = dot(grad_out, values)
    row_delta = jnp.sum(attn_weights * grad_prob, axis=1, keepdims=True)
    grad_score = (attn_weights * (grad_prob - row_delta) * score_scale).astype(jnp.bfloat16)
    return dot_tt(grad_score, keys).astype(jnp.bfloat16)


def heads_grad(query, keys, values, grad_out):
    size = keys.shape[0]
    heads = [slice(low, low + size) for low in range(0, query.shape[1], size)]
    grads = [head_grad(query[:, head], keys, values, grad_out[:, head]) for head in heads]
    return grads[0] if len(grads) == 1 else jnp.concatenate(grads, axis=1)


def half_of(array, second):
    half = array.shape[1] // 2
    return jnp.where(second, array[:, half:], array[:, :half])


def add_rows(grads, hidden, out):
    turned = grads.T
    step = out.shape[2]
    for block in range(out.shape[0]):
        out[block] = dot(turned, hidden[:, pl.ds(block * step, step)]).astype(out.dtype)


def query_kernel(
    hidden_hbm, weight_hbm, keys_hbm, values_hbm, grad_out_hbm,
    other, hidden, weight, query, grads,
    turned, keys, values, grad_out, hidden_sem, weight_sem, small_sem,
):
    tokens, width = hidden.shape
    step = width // LOADS
    chunks = [pl.ds(at * step, step) for at in range(LOADS)]
    weights = [
        pltpu.make_async_copy(weight_hbm.at[:, columns], weight.at[:, columns], weight_sem.at[at])
        for at, columns in enumerate(chunks)
    ]
    hiddens = [
        pltpu.make_async_copy(hidden_hbm.at[:, columns], hidden.at[:, columns], hidden_sem.at[at])
        for at, columns in enumerate(chunks)
    ]
    pairs = ((keys_hbm, keys), (values_hbm, values), (grad_out_hbm, grad_out))
    small = [pltpu.make_async_copy(*pair, small_sem.at[at]) for at, pair in enumerate(pairs)]
    for copy in weights + hiddens + small:
        copy.start()
    total = jnp.zeros((tokens, weight.shape[0]), jnp.float32)
    for at, columns in enumerate(chunks):
        weights[at].wait()
        turned[columns, :] = weight[:, columns].T
        hiddens[at].wait()
        total += dot(hidden[:, columns], turned[columns, :])
    rounded = total.astype(jnp.bfloat16)
    query[...] = rounded
    for copy in small:
        copy.wait()
    second = own_core() == 0
    found = heads_grad(half_of(rounded, second), keys[...], values[...], half_of(grad_out[...], second))
    grads[...] = found
    add_rows(found, hidden, other)


def query_and_other(blocks, hidden_in, query_weight, keys, values, grad_out):
    tokens, width = hidden_in.shape
    rows = query_weight.shape[0]
    like = lambda array: pltpu.VMEM(array.shape, array.dtype)
    operands = (hidden_in, query_weight, keys, values, grad_out)
    return pl.pallas_call(
        query_kernel,
        out_shape=(
            jax.ShapeDtypeStruct((blocks, rows // 2, width // blocks), jnp.bfloat16),
            jax.ShapeDtypeStruct((tokens, width), jnp.bfloat16),
            jax.ShapeDtypeStruct((rows, width), jnp.bfloat16),
            jax.ShapeDtypeStruct((tokens, rows), jnp.bfloat16),
            jax.ShapeDtypeStruct((tokens, rows // 2), jnp.bfloat16),
        ),
        in_specs=[ANY] * 5,
        out_specs=(WHOLE,) * 5,
        scratch_shapes=[
            pltpu.VMEM((width, rows), jnp.bfloat16),
            like(keys),
            like(values),
            like(grad_out),
            pltpu.SemaphoreType.DMA((LOADS,)),
            pltpu.SemaphoreType.DMA((LOADS,)),
            pltpu.SemaphoreType.DMA((3,)),
        ],
        compiler_params=pltpu.CompilerParams(vmem_limit_bytes=VMEM_LIMIT),
        cost_estimate=pl.CostEstimate(
            flops=3 * tokens * width * rows,
            bytes_accessed=2 * (tokens * width + rows * width),
            transcendentals=tokens * tokens,
        ),
    )(*(pltpu.with_memory_space_constraint(operand, pltpu.HBM) for operand in operands))


def own_kernel(hidden, query, others, keys, values, grad_out, own, grad_query):
    second = own_core() == 1
    grads = heads_grad(half_of(query[...], second), keys[...], values[...], half_of(grad_out[...], second))
    add_rows(grads, hidden, own)
    before = others[...]
    grad_query[...] = jnp.concatenate(
        [jnp.where(second, before, grads), jnp.where(second, grads, before)], axis=1
    )


def own_part(blocks, hidden, query, others, keys, values, grad_out):
    tokens, width = hidden.shape
    rows = query.shape[1]
    return pl.pallas_call(
        own_kernel,
        out_shape=(
            jax.ShapeDtypeStruct((blocks, rows // 2, width // blocks), jnp.bfloat16),
            jax.ShapeDtypeStruct((tokens, rows), jnp.bfloat16),
        ),
        in_specs=[WHOLE] * 6,
        out_specs=(WHOLE,) * 2,
        compiler_params=pltpu.CompilerParams(vmem_limit_bytes=24 * 1024 * 1024),
        cost_estimate=pl.CostEstimate(
            flops=tokens * width * rows, bytes_accessed=2 * tokens * width, transcendentals=tokens * tokens
        ),
    )(hidden, query, others, keys, values, grad_out)


def hidden_kernel(turn, grad_query, weight, *refs):
    out_hbm, found, sem = refs[-3:]

    @pl.when(own_core() == turn)
    def _():
        pieces, _, step = found.shape
        grads = grad_query[...]
        sent = []
        for piece in range(pieces):
            columns = pl.ds(piece * step, step)
            found[piece] = dot(grads, weight[:, columns]).astype(found.dtype)
            sent.append(pltpu.make_async_copy(found.at[piece], out_hbm.at[:, columns], sem.at[piece]))
            sent[-1].start()
        for copy in sent:
            copy.wait()


def hidden_part(turn, grad_query, weight, before=None):
    tokens, rows = grad_query.shape
    width = weight.shape[1]
    given = () if before is None else (before,)
    return pl.pallas_call(
        functools.partial(hidden_kernel, turn),
        out_shape=jax.ShapeDtypeStruct((tokens, width), jnp.bfloat16),
        in_specs=[WHOLE, WHOLE] + [ANY] * len(given),
        out_specs=ANY,
        scratch_shapes=[
            pltpu.VMEM((LOADS, tokens, width // LOADS), jnp.bfloat16),
            pltpu.SemaphoreType.DMA((LOADS,)),
        ],
        input_output_aliases={2: 0} if given else {},
        compiler_params=pltpu.CompilerParams(vmem_limit_bytes=24 * 1024 * 1024),
        cost_estimate=pl.CostEstimate(
            flops=2 * tokens * width * rows, bytes_accessed=2 * width * (tokens + rows), transcendentals=0
        ),
    )(grad_query, weight, *given)


def place_kernel(blocks, plan, *refs):
    out_hbm, sem = refs[-2:]
    half, step = refs[0].shape
    own = own_place(blocks)
    copies = []
    for at, (distance, turned) in enumerate(plan):
        rows = pl.ds(pl.multiple_of((own_core() ^ turned) * half, half), half)
        columns = pl.ds(pl.multiple_of((own ^ distance) * step, step), step)
        copies.append(pltpu.make_async_copy(refs[at], out_hbm.at[rows, columns], sem.at[at]))
        copies[-1].start()
    for copy in copies:
        copy.wait()


def place(blocks, plan, pieces, before=None):
    half, step = pieces[0].shape
    given = () if before is None else (before,)
    return pl.pallas_call(
        functools.partial(place_kernel, blocks, plan),
        out_shape=jax.ShapeDtypeStruct((2 * half, blocks * step), jnp.bfloat16),
        in_specs=[ANY] * (len(pieces) + len(given)),
        out_specs=ANY,
        scratch_shapes=[pltpu.SemaphoreType.DMA((len(pieces),))],
        input_output_aliases={len(pieces): 0} if given else {},
        compiler_params=pltpu.CompilerParams(vmem_limit_bytes=VMEM_LIMIT),
        cost_estimate=pl.CostEstimate(flops=0, bytes_accessed=4 * half * step * len(pieces), transcendentals=0),
    )(*pieces, *given)


def swap(array, step, count):
    return lax.ppermute(array, "dp", [(i, i ^ step) for i in range(count)])


def add(left, right):
    return (left.astype(jnp.float32) + right.astype(jnp.float32)).astype(jnp.bfloat16)


def gather(blocks, groups, total):
    count = len(groups) * blocks
    pieces = {0: total}
    for distance in sorted(range(1, blocks), key=lambda distance: -distance.bit_count()):
        pairs = [(group[at], group[at ^ distance]) for group in groups for at in range(blocks)]
        pieces[distance] = lax.ppermute(total, "dp", pairs)
    order = list(pieces)
    cut = max(len(order) - LAST, 1)
    result, turned = None, []
    for part in filter(None, (order[:cut], order[cut:])):
        held = lax.optimization_barrier([pieces[distance] for distance in part])
        arriving = [swap(piece, 1, count) for piece in held]
        plan = tuple((distance, 0) for distance in part) + tuple((distance, 1) for distance, _ in turned)
        result = place(blocks, plan, held + [piece for _, piece in turned], result)
        turned = list(zip(part, arriving))
    return place(blocks, tuple((distance, 1) for distance, _ in turned), [piece for _, piece in turned], result)


def per_device(count, hidden_in, query_weight, saved_keys, saved_values, grad_out):
    bits = count.bit_length() - 1
    wide = min(3, bits - 1)
    blocks = 1 << wide
    groups = [
        [high << (wide + 1) | (place ^ (high & 1) * (blocks >> 1)) << 1 | core for place in range(blocks)]
        for high in range(count >> (wide + 1))
        for core in range(2)
    ]
    given_width = hidden_in.shape[1]
    if given_width != query_weight.shape[1]:
        hidden_in = lax.all_gather(hidden_in, "tensor", axis=1, tiled=True)
    keys, values = saved_keys.T, saved_values.T
    other, hidden, weight, query, grads = query_and_other(
        blocks, hidden_in, query_weight, keys, values, grad_out
    )
    arriving = swap(other, 1, count)
    own, grad_query = own_part(blocks, hidden, query, grads, keys, values, grad_out)
    chip = add(own, arriving)
    input_terms = hidden_part(0, grad_query, weight)
    chip, input_terms = lax.optimization_barrier((chip, input_terms))
    parts = lax.all_to_all(chip, "dp", 0, 0, axis_index_groups=groups)
    total = jnp.sum(parts.astype(jnp.float32), axis=0).astype(jnp.bfloat16)
    input_terms, total = lax.optimization_barrier((input_terms, total))
    input_terms = hidden_part(1, grad_query, weight, input_terms)
    for bit in range(wide + 1, bits):
        arriving = swap(total, 3 << wide if bit == wide + 1 else 1 << bit, count)
        if bit == wide + 1:
            arriving, input_terms = lax.optimization_barrier((arriving, input_terms))
        total = add(total, arriving)
    grad_query_weight = gather(blocks, groups, total)
    if input_terms.shape[1] == given_width:
        grad_hidden = input_terms
    else:
        grad_hidden = lax.psum_scatter(input_terms, "tensor", scatter_dimension=1, tiled=True)
    return (grad_query_weight, grad_hidden)


def solution(mesh):
    count = mesh.shape["dp"]
    placed = (
        P("dp", "tensor"),
        P("tensor", None),
        P("dp", "tensor"),
        P("dp", "tensor"),
        P("dp", "tensor"),
    )
    return jax.shard_map(
        functools.partial(per_device, count),
        mesh=mesh,
        in_specs=placed,
        out_specs=(P("tensor", None), P("dp", "tensor")),
        check_vma=False,
    )
```

```python
import functools

import jax
import jax.numpy as jnp
from jax import lax
from jax.experimental import pallas as pl
from jax.experimental.pallas import tpu as pltpu
from jax.sharding import PartitionSpec as P

LOADS = 4
STORES = 8
EARLY = (0, 4, 3, 5)
VMEM_LIMIT = 40 * 1024 * 1024
ANY = pl.BlockSpec(memory_space=pl.ANY)
WHOLE = pl.BlockSpec(memory_space=pltpu.VMEM)


def own_core():
    return lax.axis_index("dp") & 1


def own_place(blocks):
    index = lax.axis_index("dp") >> 1
    return (index & (blocks - 1)) ^ ((index >> (blocks.bit_length() - 1) & 1) * (blocks >> 1))


def dot(left, right):
    return jnp.dot(left, right, preferred_element_type=jnp.float32)


def dot_tt(left, right):
    return lax.dot_general(left, right, (((1,), (1,)), ((), ())), preferred_element_type=jnp.float32)


def head_grad(query, keys, values, grad_out):
    head_size, length = keys.shape
    score_scale = head_size ** (-0.5)
    causal_mask = lax.broadcasted_iota(jnp.int32, (length, length), 1) <= lax.broadcasted_iota(
        jnp.int32, (length, length), 0
    )
    scores = jnp.where(causal_mask, dot(query, keys) * score_scale, -1e30)
    raised = jnp.exp(scores - jnp.max(scores, axis=1, keepdims=True))
    attn_weights = raised * (1.0 / jnp.sum(raised, axis=1, keepdims=True))
    grad_prob = dot(grad_out, values)
    row_delta = jnp.sum(attn_weights * grad_prob, axis=1, keepdims=True)
    grad_score = (attn_weights * (grad_prob - row_delta) * score_scale).astype(jnp.bfloat16)
    return dot_tt(grad_score, keys).astype(jnp.bfloat16)


def heads_grad(query, keys, values, grad_out):
    size = keys.shape[0]
    heads = [slice(low, low + size) for low in range(0, query.shape[1], size)]
    grads = [head_grad(query[:, head], keys, values, grad_out[:, head]) for head in heads]
    return grads[0] if len(grads) == 1 else jnp.concatenate(grads, axis=1)


def half_of(array, second):
    half = array.shape[1] // 2
    return jnp.where(second, array[:, half:], array[:, :half])


def add_rows(grads, hidden, out):
    turned = grads.T
    step = out.shape[2]
    for block in range(out.shape[0]):
        out[block] = dot(turned, hidden[:, pl.ds(block * step, step)]).astype(out.dtype)


def query_kernel(
    hidden_hbm, weight_hbm, keys_hbm, values_hbm, grad_out_hbm,
    other, hidden, weight, query, grads,
    turned, keys, values, grad_out, hidden_sem, weight_sem, small_sem,
):
    tokens, width = hidden.shape
    step = width // LOADS
    chunks = [pl.ds(at * step, step) for at in range(LOADS)]
    weights = [
        pltpu.make_async_copy(weight_hbm.at[:, columns], weight.at[:, columns], weight_sem.at[at])
        for at, columns in enumerate(chunks)
    ]
    hiddens = [
        pltpu.make_async_copy(hidden_hbm.at[:, columns], hidden.at[:, columns], hidden_sem.at[at])
        for at, columns in enumerate(chunks)
    ]
    pairs = ((keys_hbm, keys), (values_hbm, values), (grad_out_hbm, grad_out))
    small = [pltpu.make_async_copy(*pair, small_sem.at[at]) for at, pair in enumerate(pairs)]
    for copy in weights + hiddens + small:
        copy.start()
    total = jnp.zeros((tokens, weight.shape[0]), jnp.float32)
    for at, columns in enumerate(chunks):
        weights[at].wait()
        turned[columns, :] = weight[:, columns].T
        hiddens[at].wait()
        total += dot(hidden[:, columns], turned[columns, :])
    rounded = total.astype(jnp.bfloat16)
    query[...] = rounded
    for copy in small:
        copy.wait()
    second = own_core() == 0
    found = heads_grad(half_of(rounded, second), keys[...], values[...], half_of(grad_out[...], second))
    grads[...] = found
    add_rows(found, hidden, other)


def query_and_other(blocks, hidden_in, query_weight, keys, values, grad_out):
    tokens, width = hidden_in.shape
    rows = query_weight.shape[0]
    like = lambda array: pltpu.VMEM(array.shape, array.dtype)
    operands = (hidden_in, query_weight, keys, values, grad_out)
    return pl.pallas_call(
        query_kernel,
        out_shape=(
            jax.ShapeDtypeStruct((blocks, rows // 2, width // blocks), jnp.bfloat16),
            jax.ShapeDtypeStruct((tokens, width), jnp.bfloat16),
            jax.ShapeDtypeStruct((rows, width), jnp.bfloat16),
            jax.ShapeDtypeStruct((tokens, rows), jnp.bfloat16),
            jax.ShapeDtypeStruct((tokens, rows // 2), jnp.bfloat16),
        ),
        in_specs=[ANY] * 5,
        out_specs=(WHOLE,) * 5,
        scratch_shapes=[
            pltpu.VMEM((width, rows), jnp.bfloat16),
            like(keys),
            like(values),
            like(grad_out),
            pltpu.SemaphoreType.DMA((LOADS,)),
            pltpu.SemaphoreType.DMA((LOADS,)),
            pltpu.SemaphoreType.DMA((3,)),
        ],
        compiler_params=pltpu.CompilerParams(vmem_limit_bytes=VMEM_LIMIT),
        cost_estimate=pl.CostEstimate(
            flops=3 * tokens * width * rows,
            bytes_accessed=2 * (tokens * width + rows * width),
            transcendentals=tokens * tokens,
        ),
    )(*(pltpu.with_memory_space_constraint(operand, pltpu.HBM) for operand in operands))


def own_kernel(hidden, query, others, keys, values, grad_out, own, grad_query):
    second = own_core() == 1
    grads = heads_grad(half_of(query[...], second), keys[...], values[...], half_of(grad_out[...], second))
    add_rows(grads, hidden, own)
    before = others[...]
    grad_query[...] = jnp.concatenate(
        [jnp.where(second, before, grads), jnp.where(second, grads, before)], axis=1
    )


def own_part(blocks, hidden, query, others, keys, values, grad_out):
    tokens, width = hidden.shape
    rows = query.shape[1]
    return pl.pallas_call(
        own_kernel,
        out_shape=(
            jax.ShapeDtypeStruct((blocks, rows // 2, width // blocks), jnp.bfloat16),
            jax.ShapeDtypeStruct((tokens, rows), jnp.bfloat16),
        ),
        in_specs=[WHOLE] * 6,
        out_specs=(WHOLE,) * 2,
        compiler_params=pltpu.CompilerParams(vmem_limit_bytes=24 * 1024 * 1024),
        cost_estimate=pl.CostEstimate(
            flops=tokens * width * rows, bytes_accessed=2 * tokens * width, transcendentals=tokens * tokens
        ),
    )(hidden, query, others, keys, values, grad_out)


def hidden_kernel(turn, grad_query, weight, *refs):
    out_hbm, found, sem = refs[-3:]

    @pl.when(own_core() == turn)
    def _():
        pieces, _, step = found.shape
        grads = grad_query[...]
        sent = []
        for piece in range(pieces):
            columns = pl.ds(piece * step, step)
            found[piece] = dot(grads, weight[:, columns]).astype(found.dtype)
            sent.append(pltpu.make_async_copy(found.at[piece], out_hbm.at[:, columns], sem.at[piece]))
            sent[-1].start()
        for copy in sent:
            copy.wait()


def hidden_part(turn, grad_query, weight, before=None):
    tokens, rows = grad_query.shape
    width = weight.shape[1]
    given = () if before is None else (before,)
    return pl.pallas_call(
        functools.partial(hidden_kernel, turn),
        out_shape=jax.ShapeDtypeStruct((tokens, width), jnp.bfloat16),
        in_specs=[WHOLE, WHOLE] + [ANY] * len(given),
        out_specs=ANY,
        scratch_shapes=[
            pltpu.VMEM((STORES, tokens, width // STORES), jnp.bfloat16),
            pltpu.SemaphoreType.DMA((STORES,)),
        ],
        input_output_aliases={2: 0} if given else {},
        compiler_params=pltpu.CompilerParams(vmem_limit_bytes=24 * 1024 * 1024),
        cost_estimate=pl.CostEstimate(
            flops=2 * tokens * width * rows, bytes_accessed=2 * width * (tokens + rows), transcendentals=0
        ),
    )(grad_query, weight, *given)


def place_kernel(blocks, plan, *refs):
    out_hbm, sem = refs[-2:]
    half, step = refs[0].shape
    own = own_place(blocks)
    copies = []
    for at, (distance, turned) in enumerate(plan):
        rows = pl.ds(pl.multiple_of((own_core() ^ turned) * half, half), half)
        columns = pl.ds(pl.multiple_of((own ^ distance) * step, step), step)
        copies.append(pltpu.make_async_copy(refs[at], out_hbm.at[rows, columns], sem.at[at]))
        copies[-1].start()
    for copy in copies:
        copy.wait()


def place(blocks, plan, pieces, before=None):
    half, step = pieces[0].shape
    given = () if before is None else (before,)
    return pl.pallas_call(
        functools.partial(place_kernel, blocks, plan),
        out_shape=jax.ShapeDtypeStruct((2 * half, blocks * step), jnp.bfloat16),
        in_specs=[ANY] * (len(pieces) + len(given)),
        out_specs=ANY,
        scratch_shapes=[pltpu.SemaphoreType.DMA((len(pieces),))],
        input_output_aliases={len(pieces): 0} if given else {},
        compiler_params=pltpu.CompilerParams(vmem_limit_bytes=VMEM_LIMIT),
        cost_estimate=pl.CostEstimate(flops=0, bytes_accessed=4 * half * step * len(pieces), transcendentals=0),
    )(*pieces, *given)


def swap(array, step, count):
    return lax.ppermute(array, "dp", [(i, i ^ step) for i in range(count)])


def add(left, right):
    return (left.astype(jnp.float32) + right.astype(jnp.float32)).astype(jnp.bfloat16)


def gather(blocks, groups, total):
    count = len(groups) * blocks
    pieces = {0: total}
    for distance in sorted(range(1, blocks), key=lambda distance: -distance.bit_count()):
        pairs = [(group[at], group[at ^ distance]) for group in groups for at in range(blocks)]
        pieces[distance] = lax.ppermute(total, "dp", pairs)
    early = [distance for distance in EARLY if distance < blocks]
    late = [distance for distance in pieces if distance not in early]
    result = place(blocks, tuple((distance, 0) for distance in early), [pieces[distance] for distance in early])
    result, held = lax.optimization_barrier((result, [pieces[distance] for distance in early]))
    pieces.update(zip(early, held))
    turned = {distance: swap(pieces[distance], 1, count) for distance in early + late}
    for own, other in ((late, early), ([], late)):
        plan = tuple((distance, 0) for distance in own) + tuple((distance, 1) for distance in other)
        if plan:
            result = place(
                blocks, plan, [pieces[distance] for distance in own] + [turned[distance] for distance in other], result
            )
    return result


def per_device(count, hidden_in, query_weight, saved_keys, saved_values, grad_out):
    bits = count.bit_length() - 1
    wide = min(3, bits - 1)
    blocks = 1 << wide
    groups = [
        [high << (wide + 1) | (place ^ (high & 1) * (blocks >> 1)) << 1 | core for place in range(blocks)]
        for high in range(count >> (wide + 1))
        for core in range(2)
    ]
    given_width = hidden_in.shape[1]
    if given_width != query_weight.shape[1]:
        hidden_in = lax.all_gather(hidden_in, "tensor", axis=1, tiled=True)
    keys, values = saved_keys.T, saved_values.T
    other, hidden, weight, query, grads = query_and_other(
        blocks, hidden_in, query_weight, keys, values, grad_out
    )
    arriving = swap(other, 1, count)
    own, grad_query = own_part(blocks, hidden, query, grads, keys, values, grad_out)
    chip = add(own, arriving)
    input_terms = hidden_part(0, grad_query, weight)
    chip, input_terms = lax.optimization_barrier((chip, input_terms))
    parts = lax.all_to_all(chip, "dp", 0, 0, axis_index_groups=groups)
    total = jnp.sum(parts.astype(jnp.float32), axis=0).astype(jnp.bfloat16)
    input_terms, total = lax.optimization_barrier((input_terms, total))
    input_terms = hidden_part(1, grad_query, weight, input_terms)
    for bit in range(wide + 1, bits):
        arriving = swap(total, 3 << wide if bit == wide + 1 else 1 << bit, count)
        if bit == wide + 1:
            arriving, input_terms = lax.optimization_barrier((arriving, input_terms))
        total = add(total, arriving)
    grad_query_weight = gather(blocks, groups, total)
    if input_terms.shape[1] == given_width:
        grad_hidden = input_terms
    else:
        grad_hidden = lax.psum_scatter(input_terms, "tensor", scatter_dimension=1, tiled=True)
    return (grad_query_weight, grad_hidden)


def solution(mesh):
    count = mesh.shape["dp"]
    placed = (
        P("dp", "tensor"),
        P("tensor", None),
        P("dp", "tensor"),
        P("dp", "tensor"),
        P("dp", "tensor"),
    )
    return jax.shard_map(
        functools.partial(per_device, count),
        mesh=mesh,
        in_specs=placed,
        out_specs=(P("tensor", None), P("dp", "tensor")),
        check_vma=False,
    )
```

```python
import functools

import jax
import jax.numpy as jnp
from jax import lax
from jax.experimental import pallas as pl
from jax.experimental.pallas import tpu as pltpu
from jax.sharding import PartitionSpec as P

LOADS = 4
HIDDEN_PIECES = 4
VMEM_LIMIT = 40 * 1024 * 1024
ANY = pl.BlockSpec(memory_space=pl.ANY)
WHOLE = pl.BlockSpec(memory_space=pltpu.VMEM)


def own_core():
    return lax.axis_index("dp") & 1


def dot(left, right):
    return jnp.dot(left, right, preferred_element_type=jnp.float32)


def dot_tt(left, right):
    return lax.dot_general(left, right, (((1,), (1,)), ((), ())), preferred_element_type=jnp.float32)


def head_grad(query, keys, values, grad_out):
    head_size, length = keys.shape
    score_scale = head_size ** (-0.5)
    causal_mask = lax.broadcasted_iota(jnp.int32, (length, length), 1) <= lax.broadcasted_iota(
        jnp.int32, (length, length), 0
    )
    scores = jnp.where(causal_mask, dot(query, keys) * score_scale, -1e30)
    raised = jnp.exp(scores - jnp.max(scores, axis=1, keepdims=True))
    attn_weights = raised * (1.0 / jnp.sum(raised, axis=1, keepdims=True))
    grad_prob = dot(grad_out, values)
    row_delta = jnp.sum(attn_weights * grad_prob, axis=1, keepdims=True)
    grad_score = (attn_weights * (grad_prob - row_delta) * score_scale).astype(jnp.bfloat16)
    return dot_tt(grad_score, keys).astype(jnp.bfloat16)


def heads_grad(query, keys, values, grad_out):
    size = keys.shape[0]
    heads = [slice(low, low + size) for low in range(0, query.shape[1], size)]
    grads = [head_grad(query[:, head], keys, values, grad_out[:, head]) for head in heads]
    return grads[0] if len(grads) == 1 else jnp.concatenate(grads, axis=1)


def half_of(array, second):
    half = array.shape[1] // 2
    return jnp.where(second, array[:, half:], array[:, :half])


def add_rows(grads, hidden, out):
    turned = grads.T
    step = out.shape[2]
    for block in range(out.shape[0]):
        out[block] = dot(turned, hidden[:, pl.ds(block * step, step)]).astype(out.dtype)


def query_kernel(
    hidden_hbm, weight_hbm, keys_hbm, values_hbm, grad_out_hbm,
    other, hidden, weight, query, grads,
    turned, keys, values, grad_out, hidden_sem, weight_sem, small_sem,
):
    tokens, width = hidden.shape
    step = width // LOADS
    chunks = [pl.ds(at * step, step) for at in range(LOADS)]
    weights = [
        pltpu.make_async_copy(weight_hbm.at[:, columns], weight.at[:, columns], weight_sem.at[at])
        for at, columns in enumerate(chunks)
    ]
    hiddens = [
        pltpu.make_async_copy(hidden_hbm.at[:, columns], hidden.at[:, columns], hidden_sem.at[at])
        for at, columns in enumerate(chunks)
    ]
    pairs = ((keys_hbm, keys), (values_hbm, values), (grad_out_hbm, grad_out))
    small = [pltpu.make_async_copy(*pair, small_sem.at[at]) for at, pair in enumerate(pairs)]
    for copy in weights + hiddens + small:
        copy.start()
    total = jnp.zeros((tokens, weight.shape[0]), jnp.float32)
    for at, columns in enumerate(chunks):
        weights[at].wait()
        turned[columns, :] = weight[:, columns].T
        hiddens[at].wait()
        total += dot(hidden[:, columns], turned[columns, :])
    rounded = total.astype(jnp.bfloat16)
    query[...] = rounded
    for copy in small:
        copy.wait()
    second = own_core() == 0
    found = heads_grad(half_of(rounded, second), keys[...], values[...], half_of(grad_out[...], second))
    grads[...] = found
    add_rows(found, hidden, other)


def query_and_other(blocks, hidden_in, query_weight, keys, values, grad_out):
    tokens, width = hidden_in.shape
    rows = query_weight.shape[0]
    like = lambda array: pltpu.VMEM(array.shape, array.dtype)
    operands = (hidden_in, query_weight, keys, values, grad_out)
    return pl.pallas_call(
        query_kernel,
        out_shape=(
            jax.ShapeDtypeStruct((blocks, rows // 2, width // blocks), jnp.bfloat16),
            jax.ShapeDtypeStruct((tokens, width), jnp.bfloat16),
            jax.ShapeDtypeStruct((rows, width), jnp.bfloat16),
            jax.ShapeDtypeStruct((tokens, rows), jnp.bfloat16),
            jax.ShapeDtypeStruct((tokens, rows // 2), jnp.bfloat16),
        ),
        in_specs=[ANY] * 5,
        out_specs=(WHOLE,) * 5,
        scratch_shapes=[
            pltpu.VMEM((width, rows), jnp.bfloat16),
            like(keys),
            like(values),
            like(grad_out),
            pltpu.SemaphoreType.DMA((LOADS,)),
            pltpu.SemaphoreType.DMA((LOADS,)),
            pltpu.SemaphoreType.DMA((3,)),
        ],
        compiler_params=pltpu.CompilerParams(vmem_limit_bytes=VMEM_LIMIT),
        cost_estimate=pl.CostEstimate(
            flops=3 * tokens * width * rows,
            bytes_accessed=2 * (tokens * width + rows * width),
            transcendentals=tokens * tokens,
        ),
    )(*(pltpu.with_memory_space_constraint(operand, pltpu.HBM) for operand in operands))


def own_kernel(hidden, query, others, keys, values, grad_out, own, grad_query):
    second = own_core() == 1
    grads = heads_grad(half_of(query[...], second), keys[...], values[...], half_of(grad_out[...], second))
    add_rows(grads, hidden, own)
    before = others[...]
    grad_query[...] = jnp.concatenate(
        [jnp.where(second, before, grads), jnp.where(second, grads, before)], axis=1
    )


def own_part(blocks, hidden, query, others, keys, values, grad_out):
    tokens, width = hidden.shape
    rows = query.shape[1]
    return pl.pallas_call(
        own_kernel,
        out_shape=(
            jax.ShapeDtypeStruct((blocks, rows // 2, width // blocks), jnp.bfloat16),
            jax.ShapeDtypeStruct((tokens, rows), jnp.bfloat16),
        ),
        in_specs=[WHOLE] * 6,
        out_specs=(WHOLE,) * 2,
        compiler_params=pltpu.CompilerParams(vmem_limit_bytes=24 * 1024 * 1024),
        cost_estimate=pl.CostEstimate(
            flops=tokens * width * rows, bytes_accessed=2 * tokens * width, transcendentals=tokens * tokens
        ),
    )(hidden, query, others, keys, values, grad_out)


def hidden_kernel(turn, grad_query, weight_hbm, *refs):
    out_hbm, weight, found, load_sem, store_sem = refs[-5:]

    @pl.when(own_core() == turn)
    def _():
        width = weight.shape[1]
        loads = []
        for at in range(HIDDEN_PIECES):
            columns = pl.ds(at * (width // HIDDEN_PIECES), width // HIDDEN_PIECES)
            loads.append(pltpu.make_async_copy(weight_hbm.at[:, columns], weight.at[:, columns], load_sem.at[at]))
            loads[-1].start()
        grads = grad_query[...]
        sent = []
        for at in range(HIDDEN_PIECES):
            columns = pl.ds(at * (width // HIDDEN_PIECES), width // HIDDEN_PIECES)
            loads[at].wait()
            found[at] = dot(grads, weight[:, columns]).astype(found.dtype)
            sent.append(pltpu.make_async_copy(found.at[at], out_hbm.at[:, columns], store_sem.at[at]))
            sent[-1].start()
        for copy in sent:
            copy.wait()


def hidden_part(turn, grad_query, query_weight, before=None):
    tokens, rows = grad_query.shape
    width = query_weight.shape[1]
    given = () if before is None else (before,)
    return pl.pallas_call(
        functools.partial(hidden_kernel, turn),
        out_shape=jax.ShapeDtypeStruct((tokens, width), jnp.bfloat16),
        in_specs=[WHOLE, ANY] + [ANY] * len(given),
        out_specs=ANY,
        scratch_shapes=[
            pltpu.VMEM((rows, width), jnp.bfloat16),
            pltpu.VMEM((HIDDEN_PIECES, tokens, width // HIDDEN_PIECES), jnp.bfloat16),
            pltpu.SemaphoreType.DMA((HIDDEN_PIECES,)),
            pltpu.SemaphoreType.DMA((HIDDEN_PIECES,)),
        ],
        input_output_aliases={2: 0} if given else {},
        compiler_params=pltpu.CompilerParams(vmem_limit_bytes=24 * 1024 * 1024),
        cost_estimate=pl.CostEstimate(
            flops=2 * tokens * width * rows, bytes_accessed=2 * width * (tokens + rows), transcendentals=0
        ),
    )(grad_query, pltpu.with_memory_space_constraint(query_weight, pltpu.HBM), *given)


def place_kernel(turned, piece_hbm, *refs):
    out_hbm, sem = refs[-2:]
    blocks, half, step = piece_hbm.shape
    rows = pl.ds(pl.multiple_of((own_core() ^ turned) * half, half), half)
    copies = [
        pltpu.make_async_copy(piece_hbm.at[block], out_hbm.at[rows, pl.ds(block * step, step)], sem.at[block])
        for block in range(blocks)
    ]
    for copy in copies:
        copy.start()
    for copy in copies:
        copy.wait()


def place(turned, piece, before=None):
    blocks, half, step = piece.shape
    return pl.pallas_call(
        functools.partial(place_kernel, turned),
        out_shape=jax.ShapeDtypeStruct((2 * half, blocks * step), jnp.bfloat16),
        in_specs=[ANY] + [ANY] * (before is not None),
        out_specs=ANY,
        scratch_shapes=[pltpu.SemaphoreType.DMA((blocks,))],
        input_output_aliases={} if before is None else {1: 0},
        compiler_params=pltpu.CompilerParams(vmem_limit_bytes=VMEM_LIMIT),
        cost_estimate=pl.CostEstimate(flops=0, bytes_accessed=4 * half * blocks * step, transcendentals=0),
    )(piece, *(() if before is None else (before,)))


def swap(array, step, count):
    return lax.ppermute(array, "dp", [(i, i ^ step) for i in range(count)])


def add(left, right):
    return (left.astype(jnp.float32) + right.astype(jnp.float32)).astype(jnp.bfloat16)


def per_device(count, hidden_in, query_weight, saved_keys, saved_values, grad_out):
    bits = count.bit_length() - 1
    wide = min(3, bits - 1)
    blocks = 1 << wide
    groups = [
        [high << (wide + 1) | (place ^ (high & 1) * (blocks >> 1)) << 1 | core for place in reversed(range(blocks))]
        for high in range(count >> (wide + 1))
        for core in range(2)
    ]
    given_width = hidden_in.shape[1]
    if given_width != query_weight.shape[1]:
        hidden_in = lax.all_gather(hidden_in, "tensor", axis=1, tiled=True)
    keys, values = saved_keys.T, saved_values.T
    other, hidden, weight, query, grads = query_and_other(
        blocks, hidden_in, query_weight, keys, values, grad_out
    )
    arriving = swap(other, 1, count)
    own, grad_query = own_part(blocks, hidden, query, grads, keys, values, grad_out)
    chip = add(own, arriving)
    input_terms = hidden_part(0, grad_query, query_weight)
    chip, input_terms = lax.optimization_barrier((chip, input_terms))
    parts = lax.all_to_all(chip, "dp", 0, 0, axis_index_groups=groups)
    total = jnp.sum(parts.astype(jnp.float32), axis=0).astype(jnp.bfloat16)
    input_terms, total = lax.optimization_barrier((input_terms, total))
    input_terms = hidden_part(1, grad_query, query_weight, input_terms)
    for bit in range(wide + 1, bits):
        arriving = swap(total, 3 << wide if bit == wide + 1 else 1 << bit, count)
        if bit == wide + 1:
            arriving, input_terms = lax.optimization_barrier((arriving, input_terms))
        total = add(total, arriving)
    copies = jnp.broadcast_to(total[None], (blocks, *total.shape))
    gathered = lax.all_to_all(copies, "dp", 0, 0, axis_index_groups=groups)
    arriving = swap(gathered, 1, count)
    grad_query_weight = place(1, arriving, place(0, gathered))
    if input_terms.shape[1] == given_width:
        grad_hidden = input_terms
    else:
        grad_hidden = lax.psum_scatter(input_terms, "tensor", scatter_dimension=1, tiled=True)
    return (grad_query_weight, grad_hidden)


def solution(mesh):
    count = mesh.shape["dp"]
    placed = (
        P("dp", "tensor"),
        P("tensor", None),
        P("dp", "tensor"),
        P("dp", "tensor"),
        P("dp", "tensor"),
    )
    return jax.shard_map(
        functools.partial(per_device, count),
        mesh=mesh,
        in_specs=placed,
        out_specs=(P("tensor", None), P("dp", "tensor")),
        check_vma=False,
    )
```

```python
import functools

import jax
import jax.numpy as jnp
from jax import lax
from jax.experimental import pallas as pl
from jax.experimental.pallas import tpu as pltpu
from jax.sharding import PartitionSpec as P

LOADS = 4
PARTS = 4
HIDDEN_PIECES = 4
VMEM_LIMIT = 40 * 1024 * 1024
ANY = pl.BlockSpec(memory_space=pl.ANY)
WHOLE = pl.BlockSpec(memory_space=pltpu.VMEM)


def own_core():
    return lax.axis_index("dp") & 1


def dot(left, right):
    return jnp.dot(left, right, preferred_element_type=jnp.float32)


def dot_tt(left, right):
    return lax.dot_general(left, right, (((1,), (1,)), ((), ())), preferred_element_type=jnp.float32)


def head_grad(query, keys, values, grad_out):
    head_size, length = keys.shape
    score_scale = head_size ** (-0.5)
    causal_mask = lax.broadcasted_iota(jnp.int32, (length, length), 1) <= lax.broadcasted_iota(
        jnp.int32, (length, length), 0
    )
    scores = jnp.where(causal_mask, dot(query, keys) * score_scale, -1e30)
    raised = jnp.exp(scores - jnp.max(scores, axis=1, keepdims=True))
    attn_weights = raised * (1.0 / jnp.sum(raised, axis=1, keepdims=True))
    grad_prob = dot(grad_out, values)
    row_delta = jnp.sum(attn_weights * grad_prob, axis=1, keepdims=True)
    grad_score = (attn_weights * (grad_prob - row_delta) * score_scale).astype(jnp.bfloat16)
    return dot_tt(grad_score, keys).astype(jnp.bfloat16)


def heads_grad(query, keys, values, grad_out):
    size = keys.shape[0]
    heads = [slice(low, low + size) for low in range(0, query.shape[1], size)]
    grads = [head_grad(query[:, head], keys, values, grad_out[:, head]) for head in heads]
    return grads[0] if len(grads) == 1 else jnp.concatenate(grads, axis=1)


def half_of(array, second):
    half = array.shape[1] // 2
    return jnp.where(second, array[:, half:], array[:, :half])


def add_rows(grads, hidden, out):
    turned = grads.T
    step = out.shape[1] // PARTS
    for part in range(PARTS):
        columns = pl.ds(part * step, step)
        out[:, columns] = dot(turned, hidden[:, columns]).astype(out.dtype)


def query_kernel(
    hidden_hbm, weight_hbm, keys_hbm, values_hbm, grad_out_hbm,
    other, hidden, weight, query, grads,
    turned, keys, values, grad_out, hidden_sem, weight_sem, small_sem,
):
    tokens, width = hidden.shape
    step = width // LOADS
    chunks = [pl.ds(at * step, step) for at in range(LOADS)]
    weights = [
        pltpu.make_async_copy(weight_hbm.at[:, columns], weight.at[:, columns], weight_sem.at[at])
        for at, columns in enumerate(chunks)
    ]
    hiddens = [
        pltpu.make_async_copy(hidden_hbm.at[:, columns], hidden.at[:, columns], hidden_sem.at[at])
        for at, columns in enumerate(chunks)
    ]
    pairs = ((keys_hbm, keys), (values_hbm, values), (grad_out_hbm, grad_out))
    small = [pltpu.make_async_copy(*pair, small_sem.at[at]) for at, pair in enumerate(pairs)]
    for copy in weights + hiddens + small:
        copy.start()
    total = jnp.zeros((tokens, weight.shape[0]), jnp.float32)
    for at, columns in enumerate(chunks):
        weights[at].wait()
        turned[columns, :] = weight[:, columns].T
        hiddens[at].wait()
        total += dot(hidden[:, columns], turned[columns, :])
    rounded = total.astype(jnp.bfloat16)
    query[...] = rounded
    for copy in small:
        copy.wait()
    second = own_core() == 0
    found = heads_grad(half_of(rounded, second), keys[...], values[...], half_of(grad_out[...], second))
    grads[...] = found
    add_rows(found, hidden, other)


def query_and_other(hidden_in, query_weight, keys, values, grad_out):
    tokens, width = hidden_in.shape
    rows = query_weight.shape[0]
    like = lambda array: pltpu.VMEM(array.shape, array.dtype)
    operands = (hidden_in, query_weight, keys, values, grad_out)
    return pl.pallas_call(
        query_kernel,
        out_shape=(
            jax.ShapeDtypeStruct((rows // 2, width), jnp.bfloat16),
            jax.ShapeDtypeStruct((tokens, width), jnp.bfloat16),
            jax.ShapeDtypeStruct((rows, width), jnp.bfloat16),
            jax.ShapeDtypeStruct((tokens, rows), jnp.bfloat16),
            jax.ShapeDtypeStruct((tokens, rows // 2), jnp.bfloat16),
        ),
        in_specs=[ANY] * 5,
        out_specs=(WHOLE,) * 5,
        scratch_shapes=[
            pltpu.VMEM((width, rows), jnp.bfloat16),
            like(keys),
            like(values),
            like(grad_out),
            pltpu.SemaphoreType.DMA((LOADS,)),
            pltpu.SemaphoreType.DMA((LOADS,)),
            pltpu.SemaphoreType.DMA((3,)),
        ],
        compiler_params=pltpu.CompilerParams(vmem_limit_bytes=VMEM_LIMIT),
        cost_estimate=pl.CostEstimate(
            flops=3 * tokens * width * rows,
            bytes_accessed=2 * (tokens * width + rows * width),
            transcendentals=tokens * tokens,
        ),
    )(*(pltpu.with_memory_space_constraint(operand, pltpu.HBM) for operand in operands))


def own_kernel(hidden, query, others, keys, values, grad_out, own, grad_query):
    second = own_core() == 1
    grads = heads_grad(half_of(query[...], second), keys[...], values[...], half_of(grad_out[...], second))
    add_rows(grads, hidden, own)
    before = others[...]
    grad_query[...] = jnp.concatenate(
        [jnp.where(second, before, grads), jnp.where(second, grads, before)], axis=1
    )


def own_part(hidden, query, others, keys, values, grad_out):
    tokens, width = hidden.shape
    rows = query.shape[1]
    return pl.pallas_call(
        own_kernel,
        out_shape=(
            jax.ShapeDtypeStruct((rows // 2, width), jnp.bfloat16),
            jax.ShapeDtypeStruct((tokens, rows), jnp.bfloat16),
        ),
        in_specs=[WHOLE] * 6,
        out_specs=(WHOLE,) * 2,
        compiler_params=pltpu.CompilerParams(vmem_limit_bytes=24 * 1024 * 1024),
        cost_estimate=pl.CostEstimate(
            flops=tokens * width * rows, bytes_accessed=2 * tokens * width, transcendentals=tokens * tokens
        ),
    )(hidden, query, others, keys, values, grad_out)


def hidden_kernel(turn, grad_query, weight_hbm, *refs):
    out_hbm, weight, found, load_sem, store_sem = refs[-5:]

    @pl.when(own_core() == turn)
    def _():
        width = weight.shape[1]
        loads = []
        for at in range(HIDDEN_PIECES):
            columns = pl.ds(at * (width // HIDDEN_PIECES), width // HIDDEN_PIECES)
            loads.append(pltpu.make_async_copy(weight_hbm.at[:, columns], weight.at[:, columns], load_sem.at[at]))
            loads[-1].start()
        grads = grad_query[...]
        sent = []
        for at in range(HIDDEN_PIECES):
            columns = pl.ds(at * (width // HIDDEN_PIECES), width // HIDDEN_PIECES)
            loads[at].wait()
            found[at] = dot(grads, weight[:, columns]).astype(found.dtype)
            sent.append(pltpu.make_async_copy(found.at[at], out_hbm.at[:, columns], store_sem.at[at]))
            sent[-1].start()
        for copy in sent:
            copy.wait()


def hidden_part(turn, grad_query, query_weight, before=None):
    tokens, rows = grad_query.shape
    width = query_weight.shape[1]
    given = () if before is None else (before,)
    return pl.pallas_call(
        functools.partial(hidden_kernel, turn),
        out_shape=jax.ShapeDtypeStruct((tokens, width), jnp.bfloat16),
        in_specs=[WHOLE, ANY] + [ANY] * len(given),
        out_specs=ANY,
        scratch_shapes=[
            pltpu.VMEM((rows, width), jnp.bfloat16),
            pltpu.VMEM((HIDDEN_PIECES, tokens, width // HIDDEN_PIECES), jnp.bfloat16),
            pltpu.SemaphoreType.DMA((HIDDEN_PIECES,)),
            pltpu.SemaphoreType.DMA((HIDDEN_PIECES,)),
        ],
        input_output_aliases={2: 0} if given else {},
        compiler_params=pltpu.CompilerParams(vmem_limit_bytes=24 * 1024 * 1024),
        cost_estimate=pl.CostEstimate(
            flops=2 * tokens * width * rows, bytes_accessed=2 * width * (tokens + rows), transcendentals=0
        ),
    )(grad_query, pltpu.with_memory_space_constraint(query_weight, pltpu.HBM), *given)


def place_kernel(turned, piece_hbm, *refs):
    out_hbm, sem = refs[-2:]
    half = piece_hbm.shape[0]
    rows = pl.ds(pl.multiple_of((own_core() ^ turned) * half, half), half)
    copy = pltpu.make_async_copy(piece_hbm, out_hbm.at[rows], sem)
    copy.start()
    copy.wait()


def place(turned, piece, before=None):
    half, width = piece.shape
    return pl.pallas_call(
        functools.partial(place_kernel, turned),
        out_shape=jax.ShapeDtypeStruct((2 * half, width), jnp.bfloat16),
        in_specs=[ANY] + [ANY] * (before is not None),
        out_specs=ANY,
        scratch_shapes=[pltpu.SemaphoreType.DMA(())],
        input_output_aliases={} if before is None else {1: 0},
        compiler_params=pltpu.CompilerParams(vmem_limit_bytes=VMEM_LIMIT),
        cost_estimate=pl.CostEstimate(flops=0, bytes_accessed=4 * half * width, transcendentals=0),
    )(piece, *(() if before is None else (before,)))


def swap(array, step, count):
    return lax.ppermute(array, "dp", [(i, i ^ step) for i in range(count)])


def add(left, right):
    return (left.astype(jnp.float32) + right.astype(jnp.float32)).astype(jnp.bfloat16)


def per_device(count, hidden_in, query_weight, saved_keys, saved_values, grad_out):
    bits = count.bit_length() - 1
    wide = min(3, bits - 1)
    blocks = 1 << wide
    groups = [
        [high << (wide + 1) | (place ^ (high & 1) * (blocks >> 1)) << 1 | core for place in reversed(range(blocks))]
        for high in range(count >> (wide + 1))
        for core in range(2)
    ]
    given_width = hidden_in.shape[1]
    if given_width != query_weight.shape[1]:
        hidden_in = lax.all_gather(hidden_in, "tensor", axis=1, tiled=True)
    keys, values = saved_keys.T, saved_values.T
    other, hidden, weight, query, grads = query_and_other(
        hidden_in, query_weight, keys, values, grad_out
    )
    arriving = swap(other, 1, count)
    own, grad_query = own_part(hidden, query, grads, keys, values, grad_out)
    chip = add(own, arriving)
    half, width = chip.shape
    chip = chip.reshape(blocks, half // blocks, width)
    input_terms = hidden_part(0, grad_query, query_weight)
    chip, input_terms = lax.optimization_barrier((chip, input_terms))
    parts = lax.all_to_all(chip, "dp", 0, 0, axis_index_groups=groups)
    total = jnp.sum(parts.astype(jnp.float32), axis=0).astype(jnp.bfloat16)
    input_terms, total = lax.optimization_barrier((input_terms, total))
    input_terms = hidden_part(1, grad_query, query_weight, input_terms)
    for bit in range(wide + 1, bits):
        arriving = swap(total, 3 << wide if bit == wide + 1 else 1 << bit, count)
        if bit == wide + 1:
            arriving, input_terms = lax.optimization_barrier((arriving, input_terms))
        total = add(total, arriving)
    copies = jnp.broadcast_to(total[None], (blocks, *total.shape))
    gathered = lax.all_to_all(copies, "dp", 0, 0, axis_index_groups=groups).reshape(half, width)
    arriving = swap(gathered, 1, count)
    grad_query_weight = place(1, arriving, place(0, gathered))
    if input_terms.shape[1] == given_width:
        grad_hidden = input_terms
    else:
        grad_hidden = lax.psum_scatter(input_terms, "tensor", scatter_dimension=1, tiled=True)
    return (grad_query_weight, grad_hidden)


def solution(mesh):
    count = mesh.shape["dp"]
    placed = (
        P("dp", "tensor"),
        P("tensor", None),
        P("dp", "tensor"),
        P("dp", "tensor"),
        P("dp", "tensor"),
    )
    return jax.shard_map(
        functools.partial(per_device, count),
        mesh=mesh,
        in_specs=placed,
        out_specs=(P("tensor", None), P("dp", "tensor")),
        check_vma=False,
    )
```

```python
import functools

import jax
import jax.numpy as jnp
from jax import lax
from jax.experimental import pallas as pl
from jax.experimental.pallas import tpu as pltpu
from jax.sharding import PartitionSpec as P

LOADS = 4
PARTS = 4
HIDDEN_PIECES = 4
VMEM_LIMIT = 40 * 1024 * 1024
ANY = pl.BlockSpec(memory_space=pl.ANY)
WHOLE = pl.BlockSpec(memory_space=pltpu.VMEM)


def own_core():
    return lax.axis_index("dp") & 1


def dot(left, right):
    return jnp.dot(left, right, preferred_element_type=jnp.float32)


def dot_tt(left, right):
    return lax.dot_general(left, right, (((1,), (1,)), ((), ())), preferred_element_type=jnp.float32)


def head_grad(query, keys, values, grad_out):
    head_size, length = keys.shape
    score_scale = head_size ** (-0.5)
    causal_mask = lax.broadcasted_iota(jnp.int32, (length, length), 1) <= lax.broadcasted_iota(
        jnp.int32, (length, length), 0
    )
    scores = jnp.where(causal_mask, dot(query, keys) * score_scale, -1e30)
    raised = jnp.exp(scores - jnp.max(scores, axis=1, keepdims=True))
    attn_weights = raised * (1.0 / jnp.sum(raised, axis=1, keepdims=True))
    grad_prob = dot(grad_out, values)
    row_delta = jnp.sum(attn_weights * grad_prob, axis=1, keepdims=True)
    grad_score = (attn_weights * (grad_prob - row_delta) * score_scale).astype(jnp.bfloat16)
    return dot_tt(grad_score, keys).astype(jnp.bfloat16)


def heads_grad(query, keys, values, grad_out):
    size = keys.shape[0]
    heads = [slice(low, low + size) for low in range(0, query.shape[1], size)]
    grads = [head_grad(query[:, head], keys, values, grad_out[:, head]) for head in heads]
    return grads[0] if len(grads) == 1 else jnp.concatenate(grads, axis=1)


def half_of(array, second):
    half = array.shape[1] // 2
    return jnp.where(second, array[:, half:], array[:, :half])


def add_rows(grads, hidden, out):
    turned = grads.T
    step = out.shape[1] // PARTS
    for part in range(PARTS):
        columns = pl.ds(part * step, step)
        out[:, columns] = dot(turned, hidden[:, columns]).astype(out.dtype)


def query_kernel(
    hidden_hbm, weight_hbm, keys_hbm, values_hbm, grad_out_hbm,
    other, hidden, query, grads,
    weight, turned, keys, values, grad_out, hidden_sem, weight_sem, small_sem,
):
    tokens, width = hidden.shape
    step = width // LOADS
    chunks = [pl.ds(at * step, step) for at in range(LOADS)]
    weights = [
        pltpu.make_async_copy(weight_hbm.at[:, columns], weight.at[:, columns], weight_sem.at[at])
        for at, columns in enumerate(chunks)
    ]
    hiddens = [
        pltpu.make_async_copy(hidden_hbm.at[:, columns], hidden.at[:, columns], hidden_sem.at[at])
        for at, columns in enumerate(chunks)
    ]
    pairs = ((keys_hbm, keys), (values_hbm, values), (grad_out_hbm, grad_out))
    small = [pltpu.make_async_copy(*pair, small_sem.at[at]) for at, pair in enumerate(pairs)]
    for copy in weights + hiddens + small:
        copy.start()
    total = jnp.zeros((tokens, weight.shape[0]), jnp.float32)
    for at, columns in enumerate(chunks):
        weights[at].wait()
        turned[columns, :] = weight[:, columns].T
        hiddens[at].wait()
        total += dot(hidden[:, columns], turned[columns, :])
    rounded = total.astype(jnp.bfloat16)
    query[...] = rounded
    for copy in small:
        copy.wait()
    second = own_core() == 0
    found = heads_grad(half_of(rounded, second), keys[...], values[...], half_of(grad_out[...], second))
    grads[...] = found
    add_rows(found, hidden, other)


def query_and_other(hidden_in, query_weight, keys, values, grad_out):
    tokens, width = hidden_in.shape
    rows = query_weight.shape[0]
    like = lambda array: pltpu.VMEM(array.shape, array.dtype)
    operands = (hidden_in, query_weight, keys, values, grad_out)
    return pl.pallas_call(
        query_kernel,
        out_shape=(
            jax.ShapeDtypeStruct((rows // 2, width), jnp.bfloat16),
            jax.ShapeDtypeStruct((tokens, width), jnp.bfloat16),
            jax.ShapeDtypeStruct((tokens, rows), jnp.bfloat16),
            jax.ShapeDtypeStruct((tokens, rows // 2), jnp.bfloat16),
        ),
        in_specs=[ANY] * 5,
        out_specs=(WHOLE,) * 4,
        scratch_shapes=[
            like(query_weight),
            pltpu.VMEM((width, rows), jnp.bfloat16),
            like(keys),
            like(values),
            like(grad_out),
            pltpu.SemaphoreType.DMA((LOADS,)),
            pltpu.SemaphoreType.DMA((LOADS,)),
            pltpu.SemaphoreType.DMA((3,)),
        ],
        compiler_params=pltpu.CompilerParams(vmem_limit_bytes=VMEM_LIMIT),
        cost_estimate=pl.CostEstimate(
            flops=3 * tokens * width * rows,
            bytes_accessed=2 * (tokens * width + rows * width),
            transcendentals=tokens * tokens,
        ),
    )(*(pltpu.with_memory_space_constraint(operand, pltpu.HBM) for operand in operands))


def own_kernel(hidden, query, others, keys, values, grad_out, own, grad_query):
    second = own_core() == 1
    grads = heads_grad(half_of(query[...], second), keys[...], values[...], half_of(grad_out[...], second))
    add_rows(grads, hidden, own)
    before = others[...]
    grad_query[...] = jnp.concatenate(
        [jnp.where(second, before, grads), jnp.where(second, grads, before)], axis=1
    )


def own_part(hidden, query, others, keys, values, grad_out):
    tokens, width = hidden.shape
    rows = query.shape[1]
    return pl.pallas_call(
        own_kernel,
        out_shape=(
            jax.ShapeDtypeStruct((rows // 2, width), jnp.bfloat16),
            jax.ShapeDtypeStruct((tokens, rows), jnp.bfloat16),
        ),
        in_specs=[WHOLE] * 6,
        out_specs=(WHOLE,) * 2,
        compiler_params=pltpu.CompilerParams(vmem_limit_bytes=24 * 1024 * 1024),
        cost_estimate=pl.CostEstimate(
            flops=tokens * width * rows, bytes_accessed=2 * tokens * width, transcendentals=tokens * tokens
        ),
    )(hidden, query, others, keys, values, grad_out)


def hidden_kernel(turn, grad_query, weight_hbm, *refs):
    out_hbm, weight, found, load_sem, store_sem = refs[-5:]

    @pl.when(own_core() == turn)
    def _():
        width = weight.shape[1]
        loads = []
        for at in range(HIDDEN_PIECES):
            columns = pl.ds(at * (width // HIDDEN_PIECES), width // HIDDEN_PIECES)
            loads.append(pltpu.make_async_copy(weight_hbm.at[:, columns], weight.at[:, columns], load_sem.at[at]))
            loads[-1].start()
        grads = grad_query[...]
        sent = []
        for at in range(HIDDEN_PIECES):
            columns = pl.ds(at * (width // HIDDEN_PIECES), width // HIDDEN_PIECES)
            loads[at].wait()
            found[at] = dot(grads, weight[:, columns]).astype(found.dtype)
            sent.append(pltpu.make_async_copy(found.at[at], out_hbm.at[:, columns], store_sem.at[at]))
            sent[-1].start()
        for copy in sent:
            copy.wait()


def hidden_part(turn, grad_query, query_weight, before=None):
    tokens, rows = grad_query.shape
    width = query_weight.shape[1]
    given = () if before is None else (before,)
    return pl.pallas_call(
        functools.partial(hidden_kernel, turn),
        out_shape=jax.ShapeDtypeStruct((tokens, width), jnp.bfloat16),
        in_specs=[WHOLE, ANY] + [ANY] * len(given),
        out_specs=ANY,
        scratch_shapes=[
            pltpu.VMEM((rows, width), jnp.bfloat16),
            pltpu.VMEM((HIDDEN_PIECES, tokens, width // HIDDEN_PIECES), jnp.bfloat16),
            pltpu.SemaphoreType.DMA((HIDDEN_PIECES,)),
            pltpu.SemaphoreType.DMA((HIDDEN_PIECES,)),
        ],
        input_output_aliases={2: 0} if given else {},
        compiler_params=pltpu.CompilerParams(vmem_limit_bytes=24 * 1024 * 1024),
        cost_estimate=pl.CostEstimate(
            flops=2 * tokens * width * rows, bytes_accessed=2 * width * (tokens + rows), transcendentals=0
        ),
    )(grad_query, pltpu.with_memory_space_constraint(query_weight, pltpu.HBM), *given)


def place_kernel(turned, piece_hbm, *refs):
    out_hbm, sem = refs[-2:]
    half = piece_hbm.shape[0]
    rows = pl.ds(pl.multiple_of((own_core() ^ turned) * half, half), half)
    copy = pltpu.make_async_copy(piece_hbm, out_hbm.at[rows], sem)
    copy.start()
    copy.wait()


def place(turned, piece, before=None):
    half, width = piece.shape
    return pl.pallas_call(
        functools.partial(place_kernel, turned),
        out_shape=jax.ShapeDtypeStruct((2 * half, width), jnp.bfloat16),
        in_specs=[ANY] + [ANY] * (before is not None),
        out_specs=ANY,
        scratch_shapes=[pltpu.SemaphoreType.DMA(())],
        input_output_aliases={} if before is None else {1: 0},
        compiler_params=pltpu.CompilerParams(vmem_limit_bytes=VMEM_LIMIT),
        cost_estimate=pl.CostEstimate(flops=0, bytes_accessed=4 * half * width, transcendentals=0),
    )(piece, *(() if before is None else (before,)))


def swap(array, step, count):
    return lax.ppermute(array, "dp", [(i, i ^ step) for i in range(count)])


def add(left, right):
    return (left.astype(jnp.float32) + right.astype(jnp.float32)).astype(jnp.bfloat16)


def per_device(count, hidden_in, query_weight, saved_keys, saved_values, grad_out):
    bits = count.bit_length() - 1
    wide = min(3, bits - 1)
    blocks = 1 << wide
    groups = [
        [high << (wide + 1) | (place ^ (high & 1) * (blocks >> 1)) << 1 | core for place in reversed(range(blocks))]
        for high in range(count >> (wide + 1))
        for core in range(2)
    ]
    given_width = hidden_in.shape[1]
    if given_width != query_weight.shape[1]:
        hidden_in = lax.all_gather(hidden_in, "tensor", axis=1, tiled=True)
    keys, values = saved_keys.T, saved_values.T
    other, hidden, query, grads = query_and_other(hidden_in, query_weight, keys, values, grad_out)
    arriving = swap(other, 1, count)
    own, grad_query = own_part(hidden, query, grads, keys, values, grad_out)
    chip = add(own, arriving)
    half, width = chip.shape
    chip = chip.reshape(blocks, half // blocks, width)
    input_terms = hidden_part(0, grad_query, query_weight)
    chip, input_terms = lax.optimization_barrier((chip, input_terms))
    parts = lax.all_to_all(chip, "dp", 0, 0, axis_index_groups=groups)
    total = jnp.sum(parts.astype(jnp.float32), axis=0).astype(jnp.bfloat16)
    input_terms, total = lax.optimization_barrier((input_terms, total))
    input_terms = hidden_part(1, grad_query, query_weight, input_terms)
    for bit in range(wide + 1, bits):
        arriving = swap(total, 3 << wide if bit == wide + 1 else 1 << bit, count)
        if bit == wide + 1:
            arriving, input_terms = lax.optimization_barrier((arriving, input_terms))
        total = add(total, arriving)
    copies = jnp.broadcast_to(total[None], (blocks, *total.shape))
    gathered = lax.all_to_all(copies, "dp", 0, 0, axis_index_groups=groups).reshape(half, width)
    arriving = swap(gathered, 1, count)
    grad_query_weight = place(1, arriving, place(0, gathered))
    if input_terms.shape[1] == given_width:
        grad_hidden = input_terms
    else:
        grad_hidden = lax.psum_scatter(input_terms, "tensor", scatter_dimension=1, tiled=True)
    return (grad_query_weight, grad_hidden)


def solution(mesh):
    count = mesh.shape["dp"]
    placed = (
        P("dp", "tensor"),
        P("tensor", None),
        P("dp", "tensor"),
        P("dp", "tensor"),
        P("dp", "tensor"),
    )
    return jax.shard_map(
        functools.partial(per_device, count),
        mesh=mesh,
        in_specs=placed,
        out_specs=(P("tensor", None), P("dp", "tensor")),
        check_vma=False,
    )
```

```python
import functools

import jax
import jax.numpy as jnp
from jax import lax
from jax.experimental import pallas as pl
from jax.experimental.pallas import tpu as pltpu
from jax.sharding import PartitionSpec as P

LOADS = 4
PARTS = 4
HIDDEN_PIECES = 4
VMEM_LIMIT = 40 * 1024 * 1024
ANY = pl.BlockSpec(memory_space=pl.ANY)
WHOLE = pl.BlockSpec(memory_space=pltpu.VMEM)


def own_core():
    return lax.axis_index("dp") & 1


def dot(left, right):
    return jnp.dot(left, right, preferred_element_type=jnp.float32)


def dot_tt(left, right):
    return lax.dot_general(left, right, (((1,), (1,)), ((), ())), preferred_element_type=jnp.float32)


def head_grad(query, keys, values, grad_out):
    head_size, length = keys.shape
    score_scale = head_size ** (-0.5)
    causal_mask = lax.broadcasted_iota(jnp.int32, (length, length), 1) <= lax.broadcasted_iota(
        jnp.int32, (length, length), 0
    )
    scores = jnp.where(causal_mask, dot(query, keys) * score_scale, -1e30)
    raised = jnp.exp(scores - jnp.max(scores, axis=1, keepdims=True))
    attn_weights = raised * (1.0 / jnp.sum(raised, axis=1, keepdims=True))
    grad_prob = dot(grad_out, values)
    row_delta = jnp.sum(attn_weights * grad_prob, axis=1, keepdims=True)
    grad_score = (attn_weights * (grad_prob - row_delta) * score_scale).astype(jnp.bfloat16)
    return dot_tt(grad_score, keys).astype(jnp.bfloat16)


def heads_grad(query, keys, values, grad_out):
    size = keys.shape[0]
    heads = [slice(low, low + size) for low in range(0, query.shape[1], size)]
    grads = [head_grad(query[:, head], keys, values, grad_out[:, head]) for head in heads]
    return grads[0] if len(grads) == 1 else jnp.concatenate(grads, axis=1)


def half_of(array, second):
    half = array.shape[1] // 2
    return jnp.where(second, array[:, half:], array[:, :half])


def add_rows(grads, hidden, out):
    turned = grads.T
    step = out.shape[1] // PARTS
    for part in range(PARTS):
        columns = pl.ds(part * step, step)
        out[:, columns] = dot(turned, hidden[:, columns]).astype(out.dtype)


def query_kernel(
    hidden_hbm, weight_hbm, keys_hbm, values_hbm, grad_out_hbm,
    other, hidden, query, grads,
    weight, turned, keys, values, grad_out, hidden_sem, weight_sem, small_sem,
):
    tokens, width = hidden.shape
    step = width // LOADS
    chunks = [pl.ds(at * step, step) for at in range(LOADS)]
    weights = [
        pltpu.make_async_copy(weight_hbm.at[:, columns], weight.at[:, columns], weight_sem.at[at])
        for at, columns in enumerate(chunks)
    ]
    hiddens = [
        pltpu.make_async_copy(hidden_hbm.at[:, columns], hidden.at[:, columns], hidden_sem.at[at])
        for at, columns in enumerate(chunks)
    ]
    pairs = ((keys_hbm, keys), (values_hbm, values), (grad_out_hbm, grad_out))
    small = [pltpu.make_async_copy(*pair, small_sem.at[at]) for at, pair in enumerate(pairs)]
    for copy in weights + hiddens + small:
        copy.start()
    total = jnp.zeros((tokens, weight.shape[0]), jnp.float32)
    for at, columns in enumerate(chunks):
        weights[at].wait()
        turned[columns, :] = weight[:, columns].T
        hiddens[at].wait()
        total += dot(hidden[:, columns], turned[columns, :])
    rounded = total.astype(jnp.bfloat16)
    query[...] = rounded
    for copy in small:
        copy.wait()
    second = own_core() == 0
    found = heads_grad(half_of(rounded, second), keys[...], values[...], half_of(grad_out[...], second))
    grads[...] = found
    add_rows(found, hidden, other)


def query_and_other(hidden_in, query_weight, keys, values, grad_out):
    tokens, width = hidden_in.shape
    rows = query_weight.shape[0]
    like = lambda array: pltpu.VMEM(array.shape, array.dtype)
    operands = (hidden_in, query_weight, keys, values, grad_out)
    return pl.pallas_call(
        query_kernel,
        out_shape=(
            jax.ShapeDtypeStruct((rows // 2, width), jnp.bfloat16),
            jax.ShapeDtypeStruct((tokens, width), jnp.bfloat16),
            jax.ShapeDtypeStruct((tokens, rows), jnp.bfloat16),
            jax.ShapeDtypeStruct((tokens, rows // 2), jnp.bfloat16),
        ),
        in_specs=[ANY] * 5,
        out_specs=(WHOLE,) * 4,
        scratch_shapes=[
            like(query_weight),
            pltpu.VMEM((width, rows), jnp.bfloat16),
            like(keys),
            like(values),
            like(grad_out),
            pltpu.SemaphoreType.DMA((LOADS,)),
            pltpu.SemaphoreType.DMA((LOADS,)),
            pltpu.SemaphoreType.DMA((3,)),
        ],
        compiler_params=pltpu.CompilerParams(vmem_limit_bytes=VMEM_LIMIT),
        cost_estimate=pl.CostEstimate(
            flops=3 * tokens * width * rows,
            bytes_accessed=2 * (tokens * width + rows * width),
            transcendentals=tokens * tokens,
        ),
    )(*(pltpu.with_memory_space_constraint(operand, pltpu.HBM) for operand in operands))


def own_kernel(hidden, query, others, keys, values, grad_out, own, grad_query):
    second = own_core() == 1
    grads = heads_grad(half_of(query[...], second), keys[...], values[...], half_of(grad_out[...], second))
    add_rows(grads, hidden, own)
    before = others[...]
    grad_query[...] = jnp.concatenate(
        [jnp.where(second, before, grads), jnp.where(second, grads, before)], axis=1
    )


def own_part(hidden, query, others, keys, values, grad_out):
    tokens, width = hidden.shape
    rows = query.shape[1]
    return pl.pallas_call(
        own_kernel,
        out_shape=(
            jax.ShapeDtypeStruct((rows // 2, width), jnp.bfloat16),
            jax.ShapeDtypeStruct((tokens, rows), jnp.bfloat16),
        ),
        in_specs=[WHOLE] * 6,
        out_specs=(WHOLE,) * 2,
        compiler_params=pltpu.CompilerParams(vmem_limit_bytes=24 * 1024 * 1024),
        cost_estimate=pl.CostEstimate(
            flops=tokens * width * rows, bytes_accessed=2 * tokens * width, transcendentals=tokens * tokens
        ),
    )(hidden, query, others, keys, values, grad_out)


def hidden_kernel(turn, grad_query, weight_hbm, *refs):
    out_hbm, weight, found, load_sem, store_sem = refs[-5:]

    @pl.when(own_core() == turn)
    def _():
        width = weight.shape[1]
        loads = []
        for at in range(HIDDEN_PIECES):
            columns = pl.ds(at * (width // HIDDEN_PIECES), width // HIDDEN_PIECES)
            loads.append(pltpu.make_async_copy(weight_hbm.at[:, columns], weight.at[:, columns], load_sem.at[at]))
            loads[-1].start()
        grads = grad_query[...]
        sent = []
        for at in range(HIDDEN_PIECES):
            columns = pl.ds(at * (width // HIDDEN_PIECES), width // HIDDEN_PIECES)
            loads[at].wait()
            found[at] = dot(grads, weight[:, columns]).astype(found.dtype)
            sent.append(pltpu.make_async_copy(found.at[at], out_hbm.at[:, columns], store_sem.at[at]))
            sent[-1].start()
        for copy in sent:
            copy.wait()


def hidden_part(turn, grad_query, query_weight, before=None):
    tokens, rows = grad_query.shape
    width = query_weight.shape[1]
    given = () if before is None else (before,)
    return pl.pallas_call(
        functools.partial(hidden_kernel, turn),
        out_shape=jax.ShapeDtypeStruct((tokens, width), jnp.bfloat16),
        in_specs=[WHOLE, ANY] + [ANY] * len(given),
        out_specs=ANY,
        scratch_shapes=[
            pltpu.VMEM((rows, width), jnp.bfloat16),
            pltpu.VMEM((HIDDEN_PIECES, tokens, width // HIDDEN_PIECES), jnp.bfloat16),
            pltpu.SemaphoreType.DMA((HIDDEN_PIECES,)),
            pltpu.SemaphoreType.DMA((HIDDEN_PIECES,)),
        ],
        input_output_aliases={2: 0} if given else {},
        compiler_params=pltpu.CompilerParams(vmem_limit_bytes=24 * 1024 * 1024),
        cost_estimate=pl.CostEstimate(
            flops=2 * tokens * width * rows, bytes_accessed=2 * width * (tokens + rows), transcendentals=0
        ),
    )(grad_query, pltpu.with_memory_space_constraint(query_weight, pltpu.HBM), *given)


def place_kernel(turned, piece_hbm, *refs):
    out_hbm, sem = refs[-2:]
    half = piece_hbm.shape[0]
    rows = pl.ds(pl.multiple_of((own_core() ^ turned) * half, half), half)
    copy = pltpu.make_async_copy(piece_hbm, out_hbm.at[rows], sem)
    copy.start()
    copy.wait()


def place(turned, piece, before=None):
    half, width = piece.shape
    return pl.pallas_call(
        functools.partial(place_kernel, turned),
        out_shape=jax.ShapeDtypeStruct((2 * half, width), jnp.bfloat16),
        in_specs=[ANY] + [ANY] * (before is not None),
        out_specs=ANY,
        scratch_shapes=[pltpu.SemaphoreType.DMA(())],
        input_output_aliases={} if before is None else {1: 0},
        compiler_params=pltpu.CompilerParams(vmem_limit_bytes=VMEM_LIMIT),
        cost_estimate=pl.CostEstimate(flops=0, bytes_accessed=4 * half * width, transcendentals=0),
    )(piece, *(() if before is None else (before,)))


def swap(array, step, count):
    return lax.ppermute(array, "dp", [(i, i ^ step) for i in range(count)])


def add(left, right):
    return (left.astype(jnp.float32) + right.astype(jnp.float32)).astype(jnp.bfloat16)


def per_device(count, hidden_in, query_weight, saved_keys, saved_values, grad_out):
    bits = count.bit_length() - 1
    wide = min(3, bits - 1)
    blocks = 1 << wide
    falling = list(reversed(range(blocks)))
    inward = [place for low in range(blocks // 2) for place in (blocks - 1 - low, low)] or falling
    groups = [
        [high << (wide + 1) | (place ^ (high & 1) * (blocks >> 1)) << 1 | core for place in (inward, falling)[core]]
        for high in range(count >> (wide + 1))
        for core in range(2)
    ]
    given_width = hidden_in.shape[1]
    if given_width != query_weight.shape[1]:
        hidden_in = lax.all_gather(hidden_in, "tensor", axis=1, tiled=True)
    keys, values = saved_keys.T, saved_values.T
    other, hidden, query, grads = query_and_other(hidden_in, query_weight, keys, values, grad_out)
    arriving = swap(other, 1, count)
    own, grad_query = own_part(hidden, query, grads, keys, values, grad_out)
    chip = add(own, arriving)
    half, width = chip.shape
    chip = chip.reshape(blocks, half // blocks, width)
    input_terms = hidden_part(0, grad_query, query_weight)
    chip, input_terms = lax.optimization_barrier((chip, input_terms))
    parts = lax.all_to_all(chip, "dp", 0, 0, axis_index_groups=groups)
    total = jnp.sum(parts.astype(jnp.float32), axis=0).astype(jnp.bfloat16)
    input_terms, total = lax.optimization_barrier((input_terms, total))
    input_terms = hidden_part(1, grad_query, query_weight, input_terms)
    for bit in range(wide + 1, bits):
        arriving = swap(total, 3 << wide if bit == wide + 1 else 1 << bit, count)
        if bit == wide + 1:
            arriving, input_terms = lax.optimization_barrier((arriving, input_terms))
        total = add(total, arriving)
    copies = jnp.broadcast_to(total[None], (blocks, *total.shape))
    gathered = lax.all_to_all(copies, "dp", 0, 0, axis_index_groups=groups).reshape(half, width)
    arriving = swap(gathered, 1, count)
    grad_query_weight = place(1, arriving, place(0, gathered))
    if input_terms.shape[1] == given_width:
        grad_hidden = input_terms
    else:
        grad_hidden = lax.psum_scatter(input_terms, "tensor", scatter_dimension=1, tiled=True)
    return (grad_query_weight, grad_hidden)


def solution(mesh):
    count = mesh.shape["dp"]
    placed = (
        P("dp", "tensor"),
        P("tensor", None),
        P("dp", "tensor"),
        P("dp", "tensor"),
        P("dp", "tensor"),
    )
    return jax.shard_map(
        functools.partial(per_device, count),
        mesh=mesh,
        in_specs=placed,
        out_specs=(P("tensor", None), P("dp", "tensor")),
        check_vma=False,
    )
```

```python
import functools

import jax
import jax.numpy as jnp
from jax import lax
from jax.experimental import pallas as pl
from jax.experimental.pallas import tpu as pltpu
from jax.sharding import PartitionSpec as P

LOADS = 4
PARTS = 4
HIDDEN_PIECES = 4
VMEM_LIMIT = 40 * 1024 * 1024
ANY = pl.BlockSpec(memory_space=pl.ANY)
WHOLE = pl.BlockSpec(memory_space=pltpu.VMEM)


def own_core():
    return lax.axis_index("dp") & 1


def dot(left, right):
    return jnp.dot(left, right, preferred_element_type=jnp.float32)


def dot_tt(left, right):
    return lax.dot_general(left, right, (((1,), (1,)), ((), ())), preferred_element_type=jnp.float32)


def head_grad(query, keys, values, grad_out):
    head_size, length = keys.shape
    score_scale = head_size ** (-0.5)
    causal_mask = lax.broadcasted_iota(jnp.int32, (length, length), 1) <= lax.broadcasted_iota(
        jnp.int32, (length, length), 0
    )
    scores = jnp.where(causal_mask, dot(query, keys) * score_scale, -1e30)
    raised = jnp.exp(scores - jnp.max(scores, axis=1, keepdims=True))
    attn_weights = raised * (1.0 / jnp.sum(raised, axis=1, keepdims=True))
    grad_prob = dot(grad_out, values)
    row_delta = jnp.sum(attn_weights * grad_prob, axis=1, keepdims=True)
    grad_score = (attn_weights * (grad_prob - row_delta) * score_scale).astype(jnp.bfloat16)
    return dot_tt(grad_score, keys).astype(jnp.bfloat16)


def heads_grad(query, keys, values, grad_out):
    size = keys.shape[0]
    heads = [slice(low, low + size) for low in range(0, query.shape[1], size)]
    grads = [head_grad(query[:, head], keys, values, grad_out[:, head]) for head in heads]
    return grads[0] if len(grads) == 1 else jnp.concatenate(grads, axis=1)


def half_of(array, second):
    half = array.shape[1] // 2
    return jnp.where(second, array[:, half:], array[:, :half])


def add_rows(grads, hidden, out):
    turned = grads.T
    step = out.shape[1] // PARTS
    for part in range(PARTS):
        columns = pl.ds(part * step, step)
        out[:, columns] = dot(turned, hidden[:, columns]).astype(out.dtype)


def query_kernel(
    hidden_hbm, weight_hbm, keys_hbm, values_hbm, grad_out_hbm,
    other, hidden, query, grads,
    weight, turned, keys, values, grad_out, hidden_sem, weight_sem, small_sem,
):
    tokens, width = hidden.shape
    step = width // LOADS
    chunks = [pl.ds(at * step, step) for at in range(LOADS)]
    weights = [
        pltpu.make_async_copy(weight_hbm.at[:, columns], weight.at[:, columns], weight_sem.at[at])
        for at, columns in enumerate(chunks)
    ]
    hiddens = [
        pltpu.make_async_copy(hidden_hbm.at[:, columns], hidden.at[:, columns], hidden_sem.at[at])
        for at, columns in enumerate(chunks)
    ]
    pairs = ((keys_hbm, keys), (values_hbm, values), (grad_out_hbm, grad_out))
    small = [pltpu.make_async_copy(*pair, small_sem.at[at]) for at, pair in enumerate(pairs)]
    for copy in weights + hiddens + small:
        copy.start()
    total = jnp.zeros((tokens, weight.shape[0]), jnp.float32)
    for at, columns in enumerate(chunks):
        weights[at].wait()
        turned[columns, :] = weight[:, columns].T
        hiddens[at].wait()
        total += dot(hidden[:, columns], turned[columns, :])
    rounded = total.astype(jnp.bfloat16)
    query[...] = rounded
    for copy in small:
        copy.wait()
    second = own_core() == 0
    found = heads_grad(half_of(rounded, second), keys[...], values[...], half_of(grad_out[...], second))
    grads[...] = found
    add_rows(found, hidden, other)


def query_and_other(hidden_in, query_weight, keys, values, grad_out):
    tokens, width = hidden_in.shape
    rows = query_weight.shape[0]
    like = lambda array: pltpu.VMEM(array.shape, array.dtype)
    operands = (hidden_in, query_weight, keys, values, grad_out)
    return pl.pallas_call(
        query_kernel,
        out_shape=(
            jax.ShapeDtypeStruct((rows // 2, width), jnp.bfloat16),
            jax.ShapeDtypeStruct((tokens, width), jnp.bfloat16),
            jax.ShapeDtypeStruct((tokens, rows), jnp.bfloat16),
            jax.ShapeDtypeStruct((tokens, rows // 2), jnp.bfloat16),
        ),
        in_specs=[ANY] * 5,
        out_specs=(WHOLE,) * 4,
        scratch_shapes=[
            like(query_weight),
            pltpu.VMEM((width, rows), jnp.bfloat16),
            like(keys),
            like(values),
            like(grad_out),
            pltpu.SemaphoreType.DMA((LOADS,)),
            pltpu.SemaphoreType.DMA((LOADS,)),
            pltpu.SemaphoreType.DMA((3,)),
        ],
        compiler_params=pltpu.CompilerParams(vmem_limit_bytes=VMEM_LIMIT),
        cost_estimate=pl.CostEstimate(
            flops=3 * tokens * width * rows,
            bytes_accessed=2 * (tokens * width + rows * width),
            transcendentals=tokens * tokens,
        ),
    )(*(pltpu.with_memory_space_constraint(operand, pltpu.HBM) for operand in operands))


def own_kernel(hidden, query, others, keys, values, grad_out, own, grad_query):
    second = own_core() == 1
    grads = heads_grad(half_of(query[...], second), keys[...], values[...], half_of(grad_out[...], second))
    add_rows(grads, hidden, own)
    before = others[...]
    grad_query[...] = jnp.concatenate(
        [jnp.where(second, before, grads), jnp.where(second, grads, before)], axis=1
    )


def own_part(hidden, query, others, keys, values, grad_out):
    tokens, width = hidden.shape
    rows = query.shape[1]
    return pl.pallas_call(
        own_kernel,
        out_shape=(
            jax.ShapeDtypeStruct((rows // 2, width), jnp.bfloat16),
            jax.ShapeDtypeStruct((tokens, rows), jnp.bfloat16),
        ),
        in_specs=[WHOLE] * 6,
        out_specs=(WHOLE,) * 2,
        compiler_params=pltpu.CompilerParams(vmem_limit_bytes=24 * 1024 * 1024),
        cost_estimate=pl.CostEstimate(
            flops=tokens * width * rows, bytes_accessed=2 * tokens * width, transcendentals=tokens * tokens
        ),
    )(hidden, query, others, keys, values, grad_out)


def hidden_kernel(turn, grad_query, weight_hbm, *refs):
    out_hbm, weight, found, load_sem, store_sem = refs[-5:]

    @pl.when(own_core() == turn)
    def _():
        width = weight.shape[1]
        loads = []
        for at in range(HIDDEN_PIECES):
            columns = pl.ds(at * (width // HIDDEN_PIECES), width // HIDDEN_PIECES)
            loads.append(pltpu.make_async_copy(weight_hbm.at[:, columns], weight.at[:, columns], load_sem.at[at]))
            loads[-1].start()
        grads = grad_query[...]
        sent = []
        for at in range(HIDDEN_PIECES):
            columns = pl.ds(at * (width // HIDDEN_PIECES), width // HIDDEN_PIECES)
            loads[at].wait()
            found[at] = dot(grads, weight[:, columns]).astype(found.dtype)
            sent.append(pltpu.make_async_copy(found.at[at], out_hbm.at[:, columns], store_sem.at[at]))
            sent[-1].start()
        for copy in sent:
            copy.wait()


def hidden_part(turn, grad_query, query_weight, before=None):
    tokens, rows = grad_query.shape
    width = query_weight.shape[1]
    given = () if before is None else (before,)
    return pl.pallas_call(
        functools.partial(hidden_kernel, turn),
        out_shape=jax.ShapeDtypeStruct((tokens, width), jnp.bfloat16),
        in_specs=[WHOLE, ANY] + [ANY] * len(given),
        out_specs=ANY,
        scratch_shapes=[
            pltpu.VMEM((rows, width), jnp.bfloat16),
            pltpu.VMEM((HIDDEN_PIECES, tokens, width // HIDDEN_PIECES), jnp.bfloat16),
            pltpu.SemaphoreType.DMA((HIDDEN_PIECES,)),
            pltpu.SemaphoreType.DMA((HIDDEN_PIECES,)),
        ],
        input_output_aliases={2: 0} if given else {},
        compiler_params=pltpu.CompilerParams(vmem_limit_bytes=24 * 1024 * 1024),
        cost_estimate=pl.CostEstimate(
            flops=2 * tokens * width * rows, bytes_accessed=2 * width * (tokens + rows), transcendentals=0
        ),
    )(grad_query, pltpu.with_memory_space_constraint(query_weight, pltpu.HBM), *given)


def place_kernel(turned, offset, piece_hbm, *refs):
    out_hbm, sem = refs[-2:]
    half, size = out_hbm.shape[0] // 2, piece_hbm.shape[0]
    rows = pl.ds(pl.multiple_of((own_core() ^ turned) * half + offset, size), size)
    copy = pltpu.make_async_copy(piece_hbm, out_hbm.at[rows], sem)
    copy.start()
    copy.wait()


def place(turned, offset, half, piece, before=None):
    size, width = piece.shape
    return pl.pallas_call(
        functools.partial(place_kernel, turned, offset),
        out_shape=jax.ShapeDtypeStruct((2 * half, width), jnp.bfloat16),
        in_specs=[ANY] + [ANY] * (before is not None),
        out_specs=ANY,
        scratch_shapes=[pltpu.SemaphoreType.DMA(())],
        input_output_aliases={} if before is None else {1: 0},
        compiler_params=pltpu.CompilerParams(vmem_limit_bytes=VMEM_LIMIT),
        cost_estimate=pl.CostEstimate(flops=0, bytes_accessed=4 * size * width, transcendentals=0),
    )(piece, *(() if before is None else (before,)))


def swap(array, step, count):
    return lax.ppermute(array, "dp", [(i, i ^ step) for i in range(count)])


def add(left, right):
    return (left.astype(jnp.float32) + right.astype(jnp.float32)).astype(jnp.bfloat16)


def per_device(count, hidden_in, query_weight, saved_keys, saved_values, grad_out):
    bits = count.bit_length() - 1
    wide = min(3, bits - 1)
    blocks = 1 << wide
    falling = list(reversed(range(blocks)))
    inward = [place for low in range(blocks // 2) for place in (blocks - 1 - low, low)] or falling
    groups = [
        [high << (wide + 1) | (place ^ (high & 1) * (blocks >> 1)) << 1 | core for place in (inward, falling)[core]]
        for high in range(count >> (wide + 1))
        for core in range(2)
    ]
    given_width = hidden_in.shape[1]
    if given_width != query_weight.shape[1]:
        hidden_in = lax.all_gather(hidden_in, "tensor", axis=1, tiled=True)
    keys, values = saved_keys.T, saved_values.T
    other, hidden, query, grads = query_and_other(hidden_in, query_weight, keys, values, grad_out)
    arriving = swap(other, 1, count)
    own, grad_query = own_part(hidden, query, grads, keys, values, grad_out)
    chip = add(own, arriving)
    half, width = chip.shape
    chip = chip.reshape(blocks, half // blocks, width)
    input_terms = hidden_part(0, grad_query, query_weight)
    chip, input_terms = lax.optimization_barrier((chip, input_terms))
    parts = lax.all_to_all(chip, "dp", 0, 0, axis_index_groups=groups)
    total = jnp.sum(parts.astype(jnp.float32), axis=0).astype(jnp.bfloat16)
    input_terms, total = lax.optimization_barrier((input_terms, total))
    input_terms = hidden_part(1, grad_query, query_weight, input_terms)
    for bit in range(wide + 1, bits):
        arriving = swap(total, 3 << wide if bit == wide + 1 else 1 << bit, count)
        if bit == wide + 1:
            arriving, input_terms = lax.optimization_barrier((arriving, input_terms))
        total = add(total, arriving)
    copies = jnp.broadcast_to(total[None], (blocks, *total.shape))
    gathered = lax.all_to_all(copies, "dp", 0, 0, axis_index_groups=groups).reshape(half, width)
    cuts = (0, half // 2)
    arriving = [swap(gathered[cut : cut + half // 2], 1, count) for cut in cuts]
    grad_query_weight = place(0, 0, half, gathered)
    for cut, piece in zip(cuts, arriving):
        grad_query_weight = place(1, cut, half, piece, grad_query_weight)
    if input_terms.shape[1] == given_width:
        grad_hidden = input_terms
    else:
        grad_hidden = lax.psum_scatter(input_terms, "tensor", scatter_dimension=1, tiled=True)
    return (grad_query_weight, grad_hidden)


def solution(mesh):
    count = mesh.shape["dp"]
    placed = (
        P("dp", "tensor"),
        P("tensor", None),
        P("dp", "tensor"),
        P("dp", "tensor"),
        P("dp", "tensor"),
    )
    return jax.shard_map(
        functools.partial(per_device, count),
        mesh=mesh,
        in_specs=placed,
        out_specs=(P("tensor", None), P("dp", "tensor")),
        check_vma=False,
    )
```
